256 devices in a mesh: ctx: 32 (over z_lo, x, core), exp: 8 (over z_hi, y).
Axes of the slice: x: 4, y: 4, z: 8 (z_hi: 2, z_lo: 4; z = z_hi * 4 + z_lo), core: 2. Of those that a mesh axis runs over, the one named last changes fastest.
Arguments:
- residual_in: bfloat16 [2048, 4096], P('ctx', 'exp'), may hold values from -16 to 16
- queries: bfloat16 [2048, 4096], P('ctx', 'exp'), may hold values from -5 to 5
- context_key_cache: bfloat16 [32768, 1024], P('ctx', 'exp'), may hold values from -5 to 5
- context_value_cache: bfloat16 [32768, 1024], P('ctx', 'exp'), may hold values from -10 to 10
- query_pos: int32 [2048], P('ctx'), may hold values from 0 to 32767, as said below
- norm_gain: bfloat16 [4096], replicated, may hold values from 0.099609375 to 1.8984375
- w_gate: bfloat16 [8, 14336, 4096], P('exp', 'ctx'), may hold values from -0.09375 to 0.09375
- w_up: bfloat16 [8, 14336, 4096], P('exp', 'ctx'), may hold values from -0.09375 to 0.09375
- w_down: bfloat16 [8, 14336, 4096], P('exp', 'ctx'), may hold values from -0.046875 to 0.046875
- expert_ids: int32 [2048, 2], P('ctx'), may hold values from 0 to 7, as said below
- kept_choices: int32 [2048, 2], P('ctx'), may hold values from 0 to 1, as said below
- gate_weights: float32 [2048, 2], P('ctx'), may hold values from 0.1 to 0.9
Outputs:
- layer_out: bfloat16 [2048, 4096], P('ctx', 'exp')
The draws below stay inside these ranges and needn't reach their ends.
Inputs may be any that keep to these rules, and one draw needn't show every extreme that they name: `query_pos`: query token i stands at a context position from i * 16 to (i + 1) * 16 - 1. `expert_ids`: each row names 2 different experts. `kept_choices`: within each block of 64 consecutive tokens, the choices of an expert are ranked first choices before second choices and then by token, and exactly those of rank under 12 are kept; some expert keeps 12 choices from every block.
All inputs are finite; a program needn't handle non-finite values.
Results may differ from the reference program's by a relative error of at most 0.015.
Values may be sent and summed in bfloat16 or wider, within the bound.
A program may use at most 128 MiB of HBM per device.

```python
import math
import jax
import jax.numpy as jnp
from jax import lax

D = 4096
QUERY_HEADS = 32
KEY_VALUE_HEADS = 8
HEAD_WIDTH = 128
FF = 14336
TOP = 2
Q_DEV = 64
EXPERT_TOTAL = 8
QUERY_TOKENS = 2048
CONTEXT_LENGTH = 32768
STRIDE = 16
SLOTS = 12
N_CTX = 32


def routing(key):
    blocks = QUERY_TOKENS // Q_DEV
    first_key, second_random_key, third_key, fourth_key = jax.random.split(key, 4)
    starting_score = jax.random.randint(first_key, (QUERY_TOKENS, EXPERT_TOTAL), 0, 65536)
    expert_extra_score = jax.random.randint(second_random_key, (EXPERT_TOTAL,), 0, 65536)
    hot_expert = jax.random.randint(third_key, (), 0, EXPERT_TOTAL)
    rank_table = jax.vmap(lambda block_key: jax.random.permutation(block_key, Q_DEV))(jax.random.split(fourth_key, blocks))
    forced_choice = (rank_table < SLOTS).reshape(QUERY_TOKENS).astype(jnp.int32)
    column = jnp.arange(EXPERT_TOTAL, dtype=jnp.int32)
    hot_flag = (column[None, :] == hot_expert).astype(jnp.int32)
    score_value = starting_score + expert_extra_score[None, :] + forced_choice[:, None] * hot_flag * 262144
    score_value = score_value * EXPERT_TOTAL + column[None, :]
    _, chosen_ids = lax.top_k(score_value, TOP)
    chosen_ids = chosen_ids.astype(jnp.int32)
    onehot = (chosen_ids[:, :, None] == column[None, None, :]).astype(jnp.int32)
    ordered = onehot.reshape(blocks, Q_DEV, TOP, EXPERT_TOTAL).transpose(0, 2, 1, 3).reshape(blocks, TOP * Q_DEV, EXPERT_TOTAL)
    ranked = jnp.cumsum(ordered, axis=1) - ordered
    keeping = jnp.sum(ordered * (ranked < SLOTS).astype(jnp.int32), axis=2)
    keeping = keeping.reshape(blocks, TOP, Q_DEV).transpose(0, 2, 1).reshape(QUERY_TOKENS, TOP)
    return (chosen_ids, keeping.astype(jnp.int32))


def draw_expert_ids(key, part):
    return routing(key)[0]


def draw_kept_choices(key, part):
    return routing(key)[1]


def draw_query_pos(key, part):
    key = jax.random.fold_in(key, 11)
    offsets = jax.random.randint(key, (QUERY_TOKENS,), 0, STRIDE)
    offsets = offsets.at[0].set(0).at[QUERY_TOKENS - 1].set(STRIDE - 1)
    return (jnp.arange(QUERY_TOKENS, dtype=jnp.int32) * STRIDE + offsets).astype(jnp.int32)


def draw_residual_in(key, part):
    key = jax.random.fold_in(key, 3)
    row_key, col_key, noise_key = jax.random.split(key, 3)
    row_scale = jnp.exp(jax.random.uniform(row_key, (QUERY_TOKENS, 1), jnp.float32, math.log(0.5), math.log(2.0)))
    col_scale = jnp.exp(jax.random.uniform(col_key, (1, D), jnp.float32, math.log(0.5), math.log(2.0)))
    noise = jnp.clip(jax.random.normal(noise_key, (QUERY_TOKENS, D), jnp.float32), -4.0, 4.0)
    return (row_scale * col_scale * noise).astype(jnp.bfloat16)


def draw_queries(key, part):
    key = jax.random.fold_in(key, 5)
    drawn_result = jnp.clip(1.5 * jax.random.normal(key, (QUERY_TOKENS, QUERY_HEADS * HEAD_WIDTH), jnp.float32), -5.0, 5.0)
    return drawn_result.astype(jnp.bfloat16)


def draw_context_key_cache(key, part):
    key = jax.random.fold_in(key, 7)
    drawn_result = jnp.clip(1.5 * jax.random.normal(key, (CONTEXT_LENGTH, KEY_VALUE_HEADS * HEAD_WIDTH), jnp.float32), -5.0, 5.0)
    return drawn_result.astype(jnp.bfloat16)


def level_of(rng, dims, shards, low, top_value):
    loudness, own = 1.0, jax.random.fold_in(rng, 6)
    for axis_at, blocks in shards:
        steps = jnp.exp(jax.random.uniform(jax.random.fold_in(own, axis_at), (blocks,), jnp.float32, low / len(shards), top_value / len(shards)))
        loudness = loudness * jnp.repeat(steps, dims[axis_at] // blocks).reshape([-1 if axis == axis_at else 1 for axis in range(len(dims))])
    return loudness


def bell_draw(rng, shape, width, reach, cuts=(), kind=jnp.bfloat16):
    gain = level_of(rng, shape, cuts, -0.22, 0.18) if cuts else 1.0
    result = jax.random.normal(rng, shape, jnp.float32) * width * gain
    return jnp.minimum(jnp.maximum(result, -reach), reach).astype(kind)


def setup_inputs(seed: int = 0) -> dict:
    key_list = jax.random.split(jax.random.key(seed), 13)
    residual_in = draw_residual_in(jax.random.fold_in(key_list[12], 71), 0)
    queries = draw_queries(jax.random.fold_in(key_list[12], 71), 0)
    context_key_cache = draw_context_key_cache(jax.random.fold_in(key_list[12], 71), 0)
    context_value_cache = bell_draw(key_list[3], (CONTEXT_LENGTH, KEY_VALUE_HEADS * HEAD_WIDTH), 2.0, 10.0, ((0, 32), (1, 8)))
    query_pos = draw_query_pos(jax.random.fold_in(key_list[12], 71), 0)
    norm_gain = jnp.clip(1.0 + 0.18 * jax.random.normal(key_list[5], (D,), jnp.float32), 0.099609375, 1.8984375).astype(jnp.bfloat16)
    w_gate = bell_draw(key_list[6], (EXPERT_TOTAL, FF, D), D ** -0.5, 0.09375, ((0, 8), (1, 32)))
    w_up = bell_draw(key_list[7], (EXPERT_TOTAL, FF, D), D ** -0.5, 0.09375, ((0, 8), (1, 32)))
    w_down = bell_draw(key_list[8], (EXPERT_TOTAL, FF, D), FF ** -0.5, 0.046875, ((0, 8), (1, 32)))
    expert_ids = draw_expert_ids(jax.random.fold_in(key_list[12], 71), 0)
    kept_choices = draw_kept_choices(jax.random.fold_in(key_list[12], 71), 0)
    gate_weights = jnp.clip(0.1 + 0.79999997 * jax.random.uniform(key_list[11], (QUERY_TOKENS, TOP), jnp.float32) ** level_of(key_list[11], (QUERY_TOKENS, TOP), ((0, 32),), -0.2, 0.2), 0.1, 0.9)
    return dict(residual_in=residual_in, queries=queries, context_key_cache=context_key_cache, context_value_cache=context_value_cache, query_pos=query_pos, norm_gain=norm_gain, w_gate=w_gate, w_up=w_up, w_down=w_down, expert_ids=expert_ids, kept_choices=kept_choices, gate_weights=gate_weights)


NEG_FILL = -1e+30
NORM_EPS = 1e-05
FULL = lax.Precision.HIGHEST

def attend_rows(operands, key_lookup_table, value_lookup_table):
    query_tile_block, pos_block = operands
    count_of_rows = query_tile_block.shape[0]
    group_width = QUERY_HEADS // KEY_VALUE_HEADS
    reshaped_array = query_tile_block.astype(jnp.float32).reshape(count_of_rows, KEY_VALUE_HEADS, group_width, HEAD_WIDTH)
    scores = jnp.einsum('rkgd,nkd->rkgn', reshaped_array, key_lookup_table, precision=FULL) * HEAD_WIDTH ** (-0.5)
    positions = jnp.arange(CONTEXT_LENGTH, dtype=jnp.int32)
    visible = (positions[None, :] <= pos_block[:, None])[:, None, None, :]
    masked = jnp.where(visible, scores, NEG_FILL)
    peak = lax.optimization_barrier(jnp.max(masked, axis=-1, keepdims=True))
    weights = jnp.where(visible, jnp.exp(masked - peak), 0.0)
    totals = lax.optimization_barrier(jnp.sum(weights, axis=-1))
    probs = lax.optimization_barrier(weights.astype(jnp.bfloat16)).astype(jnp.float32)
    summed = jnp.einsum('rkgn,nkd->rkgd', probs, value_lookup_table, precision=FULL)
    return (summed / totals[..., None]).reshape(count_of_rows, QUERY_HEADS * HEAD_WIDTH)

def slot_tables(expert_ids, kept_choices, gate_weights, expert):
    blocks = QUERY_TOKENS // Q_DEV
    matched = ((expert_ids == expert) & (kept_choices == 1)).astype(jnp.int32)
    ordered = matched.reshape(blocks, Q_DEV, TOP).transpose(0, 2, 1).reshape(blocks, TOP * Q_DEV)
    ranked = jnp.cumsum(ordered, axis=1) - ordered
    slot_index = jnp.arange(SLOTS, dtype=jnp.int32)
    picks = ((ordered[:, None, :] == 1) & (ranked[:, None, :] == slot_index[None, :, None])).astype(jnp.float32)
    gates_ordered = gate_weights.reshape(blocks, Q_DEV, TOP).transpose(0, 2, 1).reshape(blocks, TOP * Q_DEV)
    slot_gate = lax.optimization_barrier(jnp.sum(picks * gates_ordered[:, None, :], axis=2))
    token_pick = lax.optimization_barrier(jnp.sum(picks.reshape(blocks, SLOTS, TOP, Q_DEV), axis=2))
    return (token_pick, slot_gate)

def reference(residual_in, queries, context_key_cache, context_value_cache, query_pos, norm_gain, w_gate, w_up, w_down, expert_ids, kept_choices, gate_weights):
    row_block = 16
    key_lookup_table = context_key_cache.astype(jnp.float32).reshape(CONTEXT_LENGTH, KEY_VALUE_HEADS, HEAD_WIDTH)
    value_lookup_table = context_value_cache.astype(jnp.float32).reshape(CONTEXT_LENGTH, KEY_VALUE_HEADS, HEAD_WIDTH)
    attended = lax.map(lambda operands: attend_rows(operands, key_lookup_table, value_lookup_table), (queries.reshape(QUERY_TOKENS // row_block, row_block, QUERY_HEADS * HEAD_WIDTH), query_pos.reshape(QUERY_TOKENS // row_block, row_block)))
    attended = attended.reshape(QUERY_TOKENS, D)
    hidden = (residual_in.astype(jnp.float32) + attended).astype(jnp.bfloat16)
    widened = hidden.astype(jnp.float32)
    normed = (widened * lax.rsqrt(lax.optimization_barrier(jnp.mean(widened * widened, axis=-1, keepdims=True)) + NORM_EPS) * norm_gain.astype(jnp.float32)).astype(jnp.bfloat16)
    blocks = QUERY_TOKENS // Q_DEV
    capacity = blocks * SLOTS
    slice_width = FF // N_CTX
    normed_blocks = normed.astype(jnp.float32).reshape(blocks, Q_DEV, D)

    def expert_step(mixed, operands):
        expert, gate_mat, up_mat, down_mat = operands
        token_pick, slot_gate = slot_tables(expert_ids, kept_choices, gate_weights, expert)
        selected = jnp.einsum('bst,btd->bsd', token_pick, normed_blocks, precision=FULL).astype(jnp.bfloat16).reshape(capacity, D)
        gate_part = jnp.dot(selected, gate_mat.T, preferred_element_type=jnp.float32)
        up_part = jnp.dot(selected, up_mat.T, preferred_element_type=jnp.float32)
        activated = (jax.nn.silu(gate_part) * up_part).astype(jnp.bfloat16)
        act_slices = activated.reshape(capacity, N_CTX, slice_width).transpose(1, 0, 2)
        down_slices = down_mat.reshape(N_CTX, slice_width, D)

        def slice_step(running, pair):
            act_slice, down_slice = pair
            partial_sum = jnp.dot(act_slice, down_slice, preferred_element_type=jnp.float32)
            return (running + partial_sum.astype(jnp.bfloat16).astype(jnp.float32), None)
        down, _ = lax.scan(slice_step, jnp.zeros((capacity, D), jnp.float32), (act_slices, down_slices))
        weighted = down * slot_gate.reshape(capacity)[:, None]
        returned = jnp.einsum('bst,bsd->btd', token_pick, weighted.reshape(blocks, SLOTS, D), precision=FULL)
        return (mixed + returned.reshape(QUERY_TOKENS, D), None)
    mixed, _ = lax.scan(expert_step, jnp.zeros((QUERY_TOKENS, D), jnp.float32), (jnp.arange(EXPERT_TOTAL, dtype=jnp.int32), w_gate, w_up, w_down))
    return (widened + mixed).astype(jnp.bfloat16)
```

```python
import math
import types

import jax
import jax.numpy as jnp
from jax import lax
from jax.experimental import pallas as pl
from jax.experimental.pallas import tpu as pltpu
from jax.sharding import PartitionSpec as P

BF = jnp.bfloat16
F32 = jnp.float32
MESH = pl.DeviceIdType.MESH
NT = (((1,), (1,)), ((), ()))
NN = (((1,), (0,)), ((), ()))
HEAD = 128
ROWS = 64
HEADS = 4
TALL = ROWS * HEADS
KEYS = 1024
MODEL = 4096
HIDDEN = 448
EXPERTS = 8
SLOTS = 12
PIECE = SLOTS * HEADS
WIDE = EXPERTS * HEAD
NEG = -1e30
EPS = 1e-05
SCALE = HEAD ** (-0.5) * math.log2(math.e)


class Place:
    def __init__(self):
        self.me = lax.axis_index("ctx")
        self.e = lax.axis_index("exp")
        self.z = lax.div(self.me, 8)
        self.x = lax.rem(lax.div(self.me, 2), 4)
        self.a = lax.rem(self.me, 2)
        z = self.z
        self.zk = [z, z + 1 - 2 * lax.rem(z, 2), z + 2 - 4 * lax.div(z, 2), 3 - z]
        self.xr = [self.x] + [lax.rem(self.x + r, 4) for r in (1, 2, 3)]
        self.sib = self.spot(self.z, self.x, 1 - self.a)
        self.right = self.spot(self.z, self.xr[1], self.a)
        self.left = self.spot(self.z, self.xr[3], self.a)
        self.ek = [lax.rem(self.e + j, EXPERTS) for j in range(EXPERTS)]

    def spot(self, z, x, a):
        return z * 8 + x * 2 + a

    def piece(self, k, r, a):
        return self.spot(self.zk[k], self.xr[r], a)

    def column(self, k):
        return self.spot(self.zk[k], self.x, self.a)


class Mail:
    def __init__(self, place, sems):
        self.place, self.sems, self.used, self.open = place, sems, 0, []

    def ship(self, src, dst, recv_sem, ctx=None, exp=None):
        target = {"ctx": ctx} if exp is None else {"exp": exp}
        copy = pltpu.make_async_remote_copy(
            src_ref=src,
            dst_ref=dst,
            send_sem=self.sems.at[self.used],
            recv_sem=recv_sem,
            device_id=target,
            device_id_type=MESH,
        )
        self.used += 1
        copy.start()
        self.open.append(copy)

    def drain(self):
        for copy in self.open:
            copy.wait_send()
        self.open = []


def landed(slot, recv_sem, place):
    pltpu.make_async_remote_copy(
        src_ref=slot,
        dst_ref=slot,
        send_sem=recv_sem,
        recv_sem=recv_sem,
        device_id={"ctx": place.sib},
        device_id_type=MESH,
    ).wait_recv()


def wide(x, times):
    return jnp.concatenate([x] * times, axis=1)


def greet(place, with_exp):
    barrier = pltpu.get_barrier_semaphore()
    peers = [{"ctx": c} for c in (place.sib, place.right, place.left)]
    peers += [{"ctx": place.column(k)} for k in (1, 2, 3)]
    if with_exp:
        peers += [{"exp": place.ek[j]} for j in range(1, EXPERTS)]
    for peer in peers:
        pl.semaphore_signal(barrier, inc=1, device_id=peer, device_id_type=MESH)
    pl.semaphore_wait(barrier, len(peers))


def attention(place, q_ref, k_ref, v_ref, pos_ref, s):
    z, a = place.z, place.a
    mail = Mail(place, s.kv_send)

    def q_copy(k):
        return pltpu.make_async_remote_copy(
            src_ref=q_ref,
            dst_ref=s.qg.at[z],
            send_sem=s.q_send.at[k],
            recv_sem=s.q_recv.at[z],
            device_id={"ctx": place.spot(z - k, place.x, a)},
            device_id_type=MESH,
        )

    for k in (1, 2, 3):

        @pl.when(z >= k)
        def _(k=k):
            q_copy(k).start()

    mine = place.x * 2 + a

    def unit(r, core):
        return place.xr[r] * 2 + core

    for target in (place.sib, place.right, place.left):
        mail.ship(k_ref, s.kg.at[mine], s.k_recv.at[mine], ctx=target)
    for target in (place.sib, place.right, place.left):
        mail.ship(v_ref, s.vg.at[mine], s.v_recv.at[mine], ctx=target)

    def got_k(r, core):
        u = unit(r, core)
        landed(s.kg.at[u], s.k_recv.at[u], place)
        return u

    def got_v(r, core):
        u = unit(r, core)
        landed(s.vg.at[u], s.v_recv.at[u], place)
        return u

    def pass_k(u, target):
        mail.ship(s.kg.at[u], s.kg.at[u], s.k_recv.at[u], ctx=target)

    def pass_v(u, target):
        mail.ship(s.vg.at[u], s.vg.at[u], s.v_recv.at[u], ctx=target)

    row = lax.broadcasted_iota(jnp.int32, (ROWS, ROWS), 0)
    col = lax.broadcasted_iota(jnp.int32, (ROWS, ROWS), 1)
    pos = pos_ref[...].astype(F32) - (place.me * KEYS).astype(F32)
    column = jnp.sum(jnp.where(row == col, pos, 0.0), axis=1, keepdims=True)
    pos_col = jnp.concatenate([column] * HEADS, axis=0)

    def prepare(zq, q):
        for h in range(HEADS):
            full = q[:, h * HEAD : (h + 1) * HEAD].astype(F32) * SCALE
            high = full.astype(BF)
            low = (full - high.astype(F32)).astype(BF)
            s.q2[zq, h * ROWS : (h + 1) * ROWS, :HEAD] = high
            s.q2[zq, h * ROWS : (h + 1) * ROWS, HEAD:] = low
        s.peak[zq] = jnp.full((TALL, HEAD), NEG, F32)
        s.acc[zq] = jnp.zeros((TALL, 2 * HEAD), F32)

    s.vv[:, HEAD:] = jnp.ones((KEYS, HEAD), BF)
    prepare(z, q_ref[...])

    def update(zq, masked):
        scores = lax.dot_general(s.q2[zq], s.kk[...], NT, preferred_element_type=F32)
        if masked:
            key = lax.broadcasted_iota(jnp.int32, (TALL, KEYS), 1).astype(F32)
            scores = jnp.where(key <= pos_col, scores, NEG)
        old = s.peak[zq]
        new = jnp.maximum(old, jnp.max(scores, axis=1, keepdims=True))
        probs = jnp.exp2(scores - wide(new, KEYS // HEAD)).astype(BF)
        part = jnp.dot(probs, s.vv[...], preferred_element_type=F32)
        shrink = jnp.exp2(old - new)
        s.acc[zq] = s.acc[zq] * wide(shrink, 2) + part
        s.peak[zq] = new

    def load(kr, vr):
        key = kr[...]
        s.kk[:, :HEAD] = key
        s.kk[:, HEAD:] = key
        s.vv[:, :HEAD] = vr[...]

    def others(_=None):
        def step(i, carry):
            update(z + 1 + i, False)
            return carry

        lax.fori_loop(0, 3 - z, step, 0)

    def whole(u):
        load(s.kg.at[u], s.vg.at[u])

        @pl.when(u < mine)
        def _():
            update(z, False)

        others()

    load(k_ref, v_ref)
    update(z, True)
    for k in (1, 2, 3):

        @pl.when(z + k <= 3)
        def _(k=k):
            landed(s.qg.at[z + k], s.q_recv.at[z + k], place)
            prepare(z + k, s.qg[z + k])

    others()
    u = got_k(0, 1 - a)
    got_v(0, 1 - a)
    whole(u)
    kl = got_k(3, a)
    pass_k(kl, place.right)
    pass_k(kl, place.sib)
    kr = got_k(1, a)
    pass_k(kr, place.sib)
    vr = got_v(1, a)
    pass_v(vr, place.left)
    pass_v(vr, place.sib)
    vl = got_v(3, a)
    pass_v(vl, place.sib)
    whole(kl)
    whole(kr)
    ko = got_k(2, a)
    pass_k(ko, place.sib)
    for r in (3, 1):
        u = got_k(r, 1 - a)
        got_v(r, 1 - a)
        whole(u)
    vo = got_v(2, a)
    pass_v(vo, place.sib)
    whole(ko)
    u = got_k(2, 1 - a)
    got_v(2, 1 - a)
    load(s.kg.at[u], s.vg.at[u])

    eye_r = lax.broadcasted_iota(jnp.int32, (HEAD, HEAD), 0)
    eye_c = lax.broadcasted_iota(jnp.int32, (HEAD, HEAD), 1)
    eye = eye_r == eye_c

    def back(zq):
        def part(src, dst, send, recv):
            return pltpu.make_async_remote_copy(
                src_ref=src.at[zq],
                dst_ref=dst.at[z],
                send_sem=send.at[zq],
                recv_sem=recv.at[z],
                device_id={"ctx": place.spot(zq, place.x, a)},
                device_id_type=MESH,
            )

        return (
            part(s.o_out, s.o_in, s.o_send, s.o_recv),
            part(s.l_out, s.l_in, s.l_send, s.l_recv),
        )

    def finish(i, carry):
        zq = 3 - i
        update(zq, False)
        total = s.acc[zq, :, HEAD:]
        s.o_out[zq] = (s.acc[zq, :, :HEAD] / total).astype(BF)
        level = s.peak[zq] + jnp.log2(total)
        for half in range(2):
            block = level[half * HEAD : (half + 1) * HEAD]
            s.l_out[zq, half : half + 1, :] = jnp.sum(
                jnp.where(eye, block, 0.0), axis=0, keepdims=True
            )
        for copy in back(zq):
            copy.start()
        return carry

    lax.fori_loop(0, 3 - z, finish, 0)

    @pl.when(u < mine)
    def _():
        update(z, False)

    for k in (1, 2, 3):

        @pl.when(z >= k)
        def _(k=k):
            zs = z - k
            landed(s.o_in.at[zs], s.o_recv.at[zs], place)
            landed(s.l_in.at[zs], s.l_recv.at[zs], place)
            spread = []
            for half in range(2):
                line = s.l_in[zs, half : half + 1, :]
                spread.append(jnp.sum(jnp.where(eye, line, 0.0), axis=1, keepdims=True))
            level = jnp.concatenate(spread, axis=0) + jnp.zeros((TALL, HEAD), F32)
            old = s.peak[z]
            new = jnp.maximum(old, level)
            shrink, weight = jnp.exp2(old - new), jnp.exp2(level - new)
            s.acc[z, :, :HEAD] = s.acc[z, :, :HEAD] * shrink + weight * s.o_in[zs].astype(F32)
            s.acc[z, :, HEAD:] = s.acc[z, :, HEAD:] * shrink + weight
            s.peak[z] = new

    for k in (1, 2, 3):

        @pl.when(z >= k)
        def _(k=k):
            q_copy(k).wait_send()

    def settle(i, carry):
        for copy in back(3 - i):
            copy.wait_send()
        return carry

    lax.fori_loop(0, 3 - z, settle, 0)
    mail.drain()
    return s.acc[z, :, :HEAD] / s.acc[z, :, HEAD:]


ATTEND_SCRATCH = dict(
    kg=pltpu.VMEM((8, KEYS, HEAD), BF),
    vg=pltpu.VMEM((8, KEYS, HEAD), BF),
    qg=pltpu.VMEM((4, ROWS, HEADS * HEAD), BF),
    q2=pltpu.VMEM((4, TALL, 2 * HEAD), BF),
    kk=pltpu.VMEM((KEYS, 2 * HEAD), BF),
    vv=pltpu.VMEM((KEYS, 2 * HEAD), BF),
    peak=pltpu.VMEM((4, TALL, HEAD), F32),
    acc=pltpu.VMEM((4, TALL, 2 * HEAD), F32),
    o_out=pltpu.VMEM((4, TALL, HEAD), BF),
    o_in=pltpu.VMEM((4, TALL, HEAD), BF),
    l_out=pltpu.VMEM((4, 8, HEAD), F32),
    l_in=pltpu.VMEM((4, 8, HEAD), F32),
    kv_send=pltpu.SemaphoreType.DMA((16,)),
    q_send=pltpu.SemaphoreType.DMA((4,)),
    q_recv=pltpu.SemaphoreType.DMA((4,)),
    k_recv=pltpu.SemaphoreType.DMA((8,)),
    v_recv=pltpu.SemaphoreType.DMA((8,)),
    o_send=pltpu.SemaphoreType.DMA((4,)),
    o_recv=pltpu.SemaphoreType.DMA((4,)),
    l_send=pltpu.SemaphoreType.DMA((4,)),
    l_recv=pltpu.SemaphoreType.DMA((4,)),
)


def attend_kernel(res_ref, q_ref, k_ref, v_ref, pos_ref, out_ref, *scratch):
    s = types.SimpleNamespace(**dict(zip(ATTEND_SCRATCH, scratch)))
    place = Place()
    greet(place, False)
    attended = attention(place, q_ref, k_ref, v_ref, pos_ref, s)
    for h in range(HEADS):
        res = res_ref[:, h * HEAD : (h + 1) * HEAD].astype(F32)
        out_ref[h * ROWS : (h + 1) * ROWS, :] = (res + attended[h * ROWS : (h + 1) * ROWS]).astype(BF)


def attend_call(residual_in, queries, keys, values, pos):
    vmem = pl.BlockSpec(memory_space=pltpu.VMEM)
    return pl.pallas_call(
        attend_kernel,
        out_shape=jax.ShapeDtypeStruct((TALL, HEAD), BF),
        in_specs=[vmem] * 5,
        out_specs=vmem,
        scratch_shapes=list(ATTEND_SCRATCH.values()),
        compiler_params=pltpu.CompilerParams(
            collective_id=0, has_side_effects=True, vmem_limit_bytes=40 * 2**20
        ),
        name="attend",
    )(residual_in, queries, keys, values, pos.reshape(1, ROWS))


def steps(index, edges):
    return sum((index >= edge).astype(jnp.int32) for edge in edges)


def slot_columns(ids_ref, kept_ref):
    lane = lax.broadcasted_iota(jnp.int32, (ROWS, HEAD), 1)
    flags = []
    for k in range(2):
        hit = (ids_ref[:, k : k + 1] == lane) & (kept_ref[:, k : k + 1] == 1)
        flags.append(hit.astype(F32))
    before = (
        lax.broadcasted_iota(jnp.int32, (ROWS, ROWS), 1)
        < lax.broadcasted_iota(jnp.int32, (ROWS, ROWS), 0)
    ).astype(F32)
    columns = []
    passed = jnp.zeros((1, HEAD), F32)
    for flag in flags:
        rank = passed + jnp.dot(before, flag, preferred_element_type=F32)
        passed = passed + jnp.sum(flag, axis=0, keepdims=True)
        slot = flag * (lane.astype(F32) * SLOTS + rank + 1.0)
        columns.append(jnp.sum(slot, axis=1, keepdims=True) - 1.0)
    return columns


def slot_and_head(index):
    expert = steps(index, range(PIECE, EXPERTS * PIECE, PIECE))
    within = index - expert * PIECE
    head = steps(within, range(SLOTS, PIECE, SLOTS))
    return (expert * SLOTS + within - head * SLOTS).astype(F32), head


def pick_rows(columns):
    shape = (EXPERTS * PIECE, TALL)
    slot, head = slot_and_head(lax.broadcasted_iota(jnp.int32, shape, 0))
    lane = lax.broadcasted_iota(jnp.int32, (ROWS, TALL), 1)
    group = steps(lane, range(ROWS, TALL, ROWS))
    same = lax.broadcasted_iota(jnp.int32, (ROWS, TALL), 0) == lane - group * ROWS
    hit = jnp.zeros(shape, F32)
    for column in columns:
        line = jnp.sum(jnp.where(same, column, 0.0), axis=0, keepdims=True)
        hit = hit + (line == slot).astype(F32)
    lanes = lax.broadcasted_iota(jnp.int32, shape, 1)
    hit = jnp.where(steps(lanes, range(ROWS, TALL, ROWS)) == head, hit, 0.0)
    return hit.astype(BF)


def place_rows(column):
    shape = (TALL, EXPERTS * PIECE)
    slot, head = slot_and_head(lax.broadcasted_iota(jnp.int32, shape, 1))
    tall = jnp.concatenate([column] * HEADS, axis=0)
    rows = lax.broadcasted_iota(jnp.int32, shape, 0)
    hit = (slot == tall) & (steps(rows, range(ROWS, TALL, ROWS)) == head)
    return hit.astype(F32).astype(BF)


def swap_matrix():
    side = 4 * PIECE
    row = lax.broadcasted_iota(jnp.int32, (side, side), 0)
    col = lax.broadcasted_iota(jnp.int32, (side, side), 1)
    first = steps(row, (PIECE, 2 * PIECE, 3 * PIECE))
    within = row - first * PIECE
    second = steps(within, (SLOTS, 2 * SLOTS, 3 * SLOTS))
    slot = within - second * SLOTS
    return (col == second * PIECE + first * SLOTS + slot).astype(F32).astype(BF)


def fetch_weights(gate_hbm, up_hbm, down_hbm, s):
    pairs = ((gate_hbm, s.w_gate), (up_hbm, s.w_up), (down_hbm, s.w_down))
    return [
        pltpu.make_async_copy(hbm.at[0], vmem, s.w_sem.at[i])
        for i, (hbm, vmem) in enumerate(pairs)
    ]


def experts(place, hidden, ids_ref, kept_ref, gate_ref, gain_ref, weights, s):
    a, e = place.a, place.e
    mail = Mail(place, s.send)

    columns = slot_columns(ids_ref, kept_ref)
    chosen = jnp.dot(pick_rows(columns), hidden, preferred_element_type=F32).astype(BF)
    for j in range(EXPERTS):
        s.pick[j] = chosen[j * PIECE : (j + 1) * PIECE]
    for j in range(1, EXPERTS):
        to = place.ek[j]
        mail.ship(s.pick.at[to], s.picked.at[e], s.picked_recv.at[e], exp=to)
    s.picked[e] = s.pick[e]
    swap = swap_matrix()
    ring = lax.broadcasted_iota(jnp.int32, (PIECE, PIECE), 0)
    ring = ring - SLOTS * steps(ring, (SLOTS, 2 * SLOTS, 3 * SLOTS))
    lap = lax.broadcasted_iota(jnp.int32, (PIECE, PIECE), 1)
    lap = lap - SLOTS * steps(lap, (SLOTS, 2 * SLOTS, 3 * SLOTS))
    alike = (ring == lap).astype(F32)
    place_of = [place_rows(column) for column in columns]
    for k in range(2):
        s.spread[k] = place_of[k]
    for j in range(1, EXPERTS):
        f = place.ek[j]
        landed(s.picked.at[f], s.picked_recv.at[f], place)

    squares = jnp.zeros((PIECE, HEAD), F32)
    for f in range(EXPERTS):
        x = s.picked[f].astype(F32)
        squares = squares + x * x
    squares = jnp.sum(squares, axis=1, keepdims=True) + jnp.zeros((PIECE, HEAD), F32)
    total = jnp.dot(alike, squares, precision=lax.Precision.HIGHEST, preferred_element_type=F32)
    scale = lax.rsqrt(total / MODEL + EPS)
    part = lax.broadcasted_iota(jnp.int32, (PIECE, HEAD), 0)
    part = steps(part, (SLOTS, 2 * SLOTS, 3 * SLOTS))
    me = place.me
    for f in range(EXPERTS):
        gain = gain_ref[f * HEADS : f * HEADS + 1, :]
        for h in range(1, HEADS):
            gain = jnp.where(part >= h, gain_ref[f * HEADS + h : f * HEADS + h + 1, :], gain)
        s.rows[me, :, f * HEAD : (f + 1) * HEAD] = (s.picked[f].astype(F32) * scale * gain).astype(BF)

    def forward(slot, *targets):
        for target in targets:
            mail.ship(s.rows.at[slot], s.rows.at[slot], s.rows_recv.at[slot], ctx=target)

    def got(k, r, core):
        slot = place.piece(k, r, core)
        landed(s.rows.at[slot], s.rows_recv.at[slot], place)
        return slot

    for k in (1, 2, 3):
        mail.ship(s.rows.at[me], s.rows.at[me], s.rows_recv.at[me], ctx=place.column(k))

    def fan(k):
        slot = me if k == 0 else got(k, 0, a)
        forward(slot, place.right, place.left, place.sib)

    def relay(k):
        slot = got(k, 3, a)
        if k % 2 == 0:
            forward(slot, place.right)
        forward(slot, place.sib)
        slot = got(k, 1, a)
        if k % 2 == 1:
            forward(slot, place.left)
        forward(slot, place.sib)

    def end(k):
        forward(got(k, 2, a), place.sib)

    def gather_siblings(k):
        for r in range(4):
            got(k, r, 1 - a)

    order = (2, 1, 3, 0)

    def pieces_of(batch, r):
        return [place.piece(2 * batch + k, r, core) for k in range(2) for core in range(2)]

    def arrange(batch):
        for n, r in enumerate(order):
            stack = jnp.concatenate([s.rows[slot] for slot in pieces_of(batch, r)], axis=0)
            turned = jnp.dot(swap, stack, preferred_element_type=F32).astype(BF)
            for h in range(HEADS):
                for f in range(EXPERTS):
                    at = (f * HEADS + h) * HEAD
                    s.x[n * PIECE : (n + 1) * PIECE, at : at + HEAD] = turned[
                        h * PIECE : (h + 1) * PIECE, f * HEAD : (f + 1) * HEAD
                    ]

    def middle():
        x = s.x[...]
        g = lax.dot_general(x, s.w_gate[...], NT, preferred_element_type=F32)
        u = lax.dot_general(x, s.w_up[...], NT, preferred_element_type=F32)
        s.act[...] = (g / (1.0 + jnp.exp(-g)) * u).astype(BF)

    def down():
        def block(f, carry):
            at = pl.ds(pl.multiple_of(f * 512, 512), 512)
            s.y[:, at] = jnp.dot(s.act[...], s.w_down[:, at], preferred_element_type=F32).astype(BF)
            return carry

        lax.fori_loop(0, EXPERTS, block, 0)

    def hand_over(batch):
        for n, r in enumerate(order):
            tall = []
            for h in range(HEADS):
                at = [(f * HEADS + h) * HEAD for f in range(EXPERTS)]
                tall.append(
                    jnp.concatenate([s.y[n * PIECE : (n + 1) * PIECE, i : i + HEAD] for i in at], axis=1)
                )
            stack = jnp.concatenate(tall, axis=0)
            turned = jnp.dot(swap, stack, preferred_element_type=F32).astype(BF)
            for p, slot in enumerate(pieces_of(batch, r)):
                s.sums[slot] = turned[p * PIECE : (p + 1) * PIECE]
            for k in (2 * batch, 2 * batch + 1):
                slot = place.piece(k, r, 1 - a)
                mail.ship(s.sums.at[slot], s.beside.at[k * 4 + r2(r)], s.beside_recv.at[k * 4 + r2(r)], ctx=place.sib)

    def r2(r):
        return r

    def pair(k, r, *more):
        n = k * 4 + r
        landed(s.beside.at[n], s.beside_recv.at[n], place)
        total = s.sums[place.piece(k, r, a)].astype(F32) + s.beside[n].astype(F32)
        for ref, recv in more:
            landed(ref, recv, place)
            total = total + ref[...].astype(F32)
        slot = place.piece(k, r, a)
        s.sums[slot] = total.astype(BF)
        return s.sums.at[slot]

    def reduce_far(k):
        target = place.right if k % 2 == 0 else place.left
        mail.ship(pair(k, 2), s.relayed.at[k], s.relayed_recv.at[k], ctx=target)

    def reduce_near(k):
        extra = (s.relayed.at[k], s.relayed_recv.at[k])
        plain, joined = (3, 1) if k % 2 == 0 else (1, 3)
        for r in (plain, joined):
            more = (extra,) if r == joined else ()
            src = pair(k, r, *more)
            if r == 1:
                mail.ship(src, s.from_left.at[k], s.left_recv.at[k], ctx=place.right)
            else:
                mail.ship(src, s.from_right.at[k], s.right_recv.at[k], ctx=place.left)

    def reduce_own(k):
        src = pair(k, 0, (s.from_left.at[k], s.left_recv.at[k]), (s.from_right.at[k], s.right_recv.at[k]))
        if k > 0:
            mail.ship(src, s.from_z.at[k], s.z_recv.at[k], ctx=place.column(k))

    fan(0)
    fan(1)
    relay(0)
    relay(1)
    fan(2)
    fan(3)
    end(0)
    end(1)
    gather_siblings(0)
    gather_siblings(1)
    arrange(0)
    relay(2)
    relay(3)
    for copy in weights:
        copy.wait()
    middle()
    end(2)
    end(3)
    down()
    hand_over(0)
    reduce_far(0)
    reduce_far(1)
    gather_siblings(2)
    gather_siblings(3)
    arrange(1)
    reduce_near(0)
    reduce_near(1)
    middle()
    down()
    hand_over(1)
    reduce_far(2)
    reduce_far(3)
    reduce_own(1)
    reduce_near(2)
    reduce_near(3)
    reduce_own(0)
    reduce_own(2)
    reduce_own(3)
    total = s.sums[me].astype(F32)
    for k in (1, 2, 3):
        landed(s.from_z.at[k], s.z_recv.at[k], place)
        total = total + s.from_z[k].astype(F32)
    total = total.astype(BF)
    for f in range(EXPERTS):
        s.done[f] = total[:, f * HEAD : (f + 1) * HEAD]
    for j in range(1, EXPERTS):
        to = place.ek[j]
        mail.ship(s.done.at[to], s.home.at[e], s.home_recv.at[e], exp=to)
    s.home[e] = s.done[e]
    for j in range(1, EXPERTS):
        f = place.ek[j]
        landed(s.home.at[f], s.home_recv.at[f], place)
    back = jnp.concatenate([s.home[j] for j in range(EXPERTS)], axis=0)
    mixed = jnp.zeros((TALL, HEAD), F32)
    for k in range(2):
        gate = jnp.concatenate([gate_ref[:, k : k + 1]] * HEADS, axis=0)
        mixed = mixed + gate * jnp.dot(s.spread[k], back, preferred_element_type=F32)
    mail.drain()
    return mixed


def piece_buffers(count):
    return pltpu.VMEM((count, PIECE, WIDE), BF)


EXPERT_SCRATCH = dict(
    w_gate=pltpu.VMEM((HIDDEN, MODEL), BF),
    w_up=pltpu.VMEM((HIDDEN, MODEL), BF),
    w_down=pltpu.VMEM((HIDDEN, MODEL), BF),
    w_sem=pltpu.SemaphoreType.DMA((3,)),
    pick=pltpu.VMEM((EXPERTS, PIECE, HEAD), BF),
    picked=pltpu.VMEM((EXPERTS, PIECE, HEAD), BF),
    spread=pltpu.VMEM((2, TALL, EXPERTS * PIECE), BF),
    rows=piece_buffers(32),
    x=pltpu.VMEM((4 * PIECE, MODEL), BF),
    act=pltpu.VMEM((4 * PIECE, HIDDEN), BF),
    y=pltpu.VMEM((4 * PIECE, MODEL), BF),
    sums=piece_buffers(32),
    beside=piece_buffers(16),
    relayed=piece_buffers(4),
    from_left=piece_buffers(4),
    from_right=piece_buffers(4),
    from_z=piece_buffers(4),
    done=pltpu.VMEM((EXPERTS, PIECE, HEAD), BF),
    home=pltpu.VMEM((EXPERTS, PIECE, HEAD), BF),
    send=pltpu.SemaphoreType.DMA((80,)),
    picked_recv=pltpu.SemaphoreType.DMA((EXPERTS,)),
    rows_recv=pltpu.SemaphoreType.DMA((32,)),
    beside_recv=pltpu.SemaphoreType.DMA((16,)),
    relayed_recv=pltpu.SemaphoreType.DMA((4,)),
    left_recv=pltpu.SemaphoreType.DMA((4,)),
    right_recv=pltpu.SemaphoreType.DMA((4,)),
    z_recv=pltpu.SemaphoreType.DMA((4,)),
    home_recv=pltpu.SemaphoreType.DMA((EXPERTS,)),
)


def expert_kernel(hidden_ref, ids_ref, kept_ref, gate_ref, gain_ref, wg, wu, wd, out_ref, *scratch):
    s = types.SimpleNamespace(**dict(zip(EXPERT_SCRATCH, scratch)))
    place = Place()
    weights = fetch_weights(wg, wu, wd, s)
    for copy in weights:
        copy.start()
    greet(place, True)
    hidden = hidden_ref[...]
    mixed = experts(place, hidden, ids_ref, kept_ref, gate_ref, gain_ref, weights, s)
    out = (hidden.astype(F32) + mixed).astype(BF)
    for h in range(HEADS):
        out_ref[:, h * HEAD : (h + 1) * HEAD] = out[h * ROWS : (h + 1) * ROWS]


def expert_call(hidden, ids, kept, gates, gain, w_gate, w_up, w_down):
    vmem = pl.BlockSpec(memory_space=pltpu.VMEM)
    hbm = pl.BlockSpec(memory_space=pl.ANY)
    return pl.pallas_call(
        expert_kernel,
        out_shape=jax.ShapeDtypeStruct((ROWS, HEADS * HEAD), BF),
        in_specs=[vmem] * 5 + [hbm] * 3,
        out_specs=vmem,
        scratch_shapes=list(EXPERT_SCRATCH.values()),
        compiler_params=pltpu.CompilerParams(
            collective_id=1, has_side_effects=True, vmem_limit_bytes=48 * 2**20
        ),
        name="experts",
    )(hidden, ids, kept, gates, gain.astype(F32).reshape(32, HEAD), w_gate, w_up, w_down)


def body(
    residual_in,
    queries,
    context_key_cache,
    context_value_cache,
    query_pos,
    norm_gain,
    w_gate,
    w_up,
    w_down,
    expert_ids,
    kept_choices,
    gate_weights,
):
    hidden = attend_call(residual_in, queries, context_key_cache, context_value_cache, query_pos)
    return expert_call(
        hidden, expert_ids, kept_choices, gate_weights, norm_gain, w_gate, w_up, w_down
    )


def solution(mesh):
    in_specs = (
        P("ctx", "exp"),
        P("ctx", "exp"),
        P("ctx", "exp"),
        P("ctx", "exp"),
        P("ctx"),
        P(),
        P("exp", "ctx", None),
        P("exp", "ctx", None),
        P("exp", "ctx", None),
        P("ctx", None),
        P("ctx", None),
        P("ctx", None),
    )
    out_specs = P("ctx", "exp")
    return jax.shard_map(body, mesh=mesh, in_specs=in_specs, out_specs=out_specs, check_vma=False)
```

```python
import math
import types

import jax
import jax.numpy as jnp
from jax import lax
from jax.experimental import pallas as pl
from jax.experimental.pallas import tpu as pltpu
from jax.sharding import PartitionSpec as P

BF = jnp.bfloat16
F32 = jnp.float32
MESH = pl.DeviceIdType.MESH
NT = (((1,), (1,)), ((), ()))
NN = (((1,), (0,)), ((), ()))
HEAD = 128
ROWS = 64
HEADS = 4
TALL = ROWS * HEADS
KEYS = 1024
MODEL = 4096
HIDDEN = 448
EXPERTS = 8
SLOTS = 12
PIECE = SLOTS * HEADS
WIDE = EXPERTS * HEAD
NEG = -1e30
EPS = 1e-05
SCALE = HEAD ** (-0.5) * math.log2(math.e)


class Place:
    def __init__(self):
        self.me = lax.axis_index("ctx")
        self.e = lax.axis_index("exp")
        self.z = lax.div(self.me, 8)
        self.x = lax.rem(lax.div(self.me, 2), 4)
        self.a = lax.rem(self.me, 2)
        z = self.z
        self.zk = [z, z + 1 - 2 * lax.rem(z, 2), z + 2 - 4 * lax.div(z, 2), 3 - z]
        self.xr = [self.x] + [lax.rem(self.x + r, 4) for r in (1, 2, 3)]
        self.sib = self.spot(self.z, self.x, 1 - self.a)
        self.right = self.spot(self.z, self.xr[1], self.a)
        self.left = self.spot(self.z, self.xr[3], self.a)
        self.far = self.spot(self.z, self.xr[2], self.a)
        self.ek = [lax.rem(self.e + j, EXPERTS) for j in range(EXPERTS)]

    def spot(self, z, x, a):
        return z * 8 + x * 2 + a

    def piece(self, k, r, a):
        return self.spot(self.zk[k], self.xr[r], a)

    def column(self, k):
        return self.spot(self.zk[k], self.x, self.a)


class Mail:
    def __init__(self, place, sems):
        self.place, self.sems, self.used, self.open = place, sems, 0, []

    def ship(self, ref, at, to_ref, to, recv, recv_at, ctx=None, exp=None):
        target = {"ctx": ctx} if exp is None else {"exp": exp}
        number = self.used
        self.used += 1

        def make():
            return pltpu.make_async_remote_copy(
                src_ref=ref.at[at],
                dst_ref=to_ref.at[to],
                send_sem=self.sems.at[number],
                recv_sem=recv.at[recv_at],
                device_id=target,
                device_id_type=MESH,
            )

        make().start()
        self.open.append(make)

    def drain(self):
        for make in self.open:
            make().wait_send()
        self.open = []


def landed(slot, recv_sem, place):
    pltpu.make_async_remote_copy(
        src_ref=slot,
        dst_ref=slot,
        send_sem=recv_sem,
        recv_sem=recv_sem,
        device_id={"ctx": place.sib},
        device_id_type=MESH,
    ).wait_recv()


def wide(x, times):
    return jnp.concatenate([x] * times, axis=1)


def upright(line):
    row = lax.broadcasted_iota(jnp.int32, (ROWS, ROWS), 0)
    col = lax.broadcasted_iota(jnp.int32, (ROWS, ROWS), 1)
    return jnp.sum(jnp.where(row == col, line, 0.0), axis=1, keepdims=True)


def greet(place):
    barrier = pltpu.get_barrier_semaphore()
    peers = [{"ctx": c} for c in (place.sib, place.right, place.left, place.far)]
    peers += [{"ctx": place.column(k)} for k in (1, 2, 3)]
    peers += [{"exp": place.ek[j]} for j in range(1, EXPERTS)]
    for peer in peers:
        pl.semaphore_signal(barrier, inc=1, device_id=peer, device_id_type=MESH)
    pl.semaphore_wait(barrier, len(peers))


def attention(place, s, local, aside):
    z, a = place.z, place.a
    mail = Mail(place, s.kv_send)
    units = [[x * 2, x * 2 + 1] for x in place.xr]
    own = [lax.select(a == 0, u[0], u[1]) for u in units]
    other = [lax.select(a == 0, u[1], u[0]) for u in units]
    mine = own[0]
    order = [own[0], other[0], own[3], own[1], other[3], other[1], own[2], other[2]]

    downs = [place.spot(z - k, place.x, a) for k in range(4)]
    ups = [z + k for k in range(4)]

    def q_copy(k):
        return pltpu.make_async_remote_copy(
            src_ref=s.qg.at[z],
            dst_ref=s.qg.at[z],
            send_sem=s.q_send.at[k],
            recv_sem=s.q_recv.at[z],
            device_id={"ctx": downs[k]},
            device_id_type=MESH,
        )

    def send(ref, sem, u, *targets):
        for target in targets:
            mail.ship(ref, u, ref, u, sem, u, ctx=target)

    def got_k(u):
        landed(s.kg.at[u], s.k_recv.at[u], place)

    def got_v(u):
        landed(s.vg.at[u], s.v_recv.at[u], place)

    local["k"].wait()
    send(s.kg, s.k_recv, mine, place.right, place.left, place.sib)
    local["q"].wait()
    for k in (1, 2, 3):

        @pl.when(z >= k)
        def _(k=k):
            q_copy(k).start()

    local["v"].wait()
    send(s.vg, s.v_recv, mine, place.right, place.left, place.sib)

    s.peak[...] = jnp.full((4 * TALL, HEAD), NEG, F32)
    s.acc[...] = jnp.zeros((4 * TALL, 2 * HEAD), F32)

    def prepare(zq):
        for h in range(HEADS):
            at = pl.ds(pl.multiple_of(zq * TALL + h * ROWS, ROWS), ROWS)
            s.q2[at, :] = s.qg[zq, :, h * HEAD : (h + 1) * HEAD]

    def update(rows, u, pos_col=None):
        scores = lax.dot_general(s.q2[rows], s.kg[u], NT, preferred_element_type=F32)
        if pos_col is not None:
            key = lax.broadcasted_iota(jnp.int32, (TALL, KEYS), 1).astype(F32)
            scores = jnp.where(key <= pos_col, scores, NEG)
        old = s.peak[rows]
        new = jnp.maximum(old, jnp.max(scores, axis=1, keepdims=True))
        probs = jnp.exp2((scores - wide(new, KEYS // HEAD)) * SCALE)
        shrink = jnp.exp2((old - new) * SCALE)
        lanes = sum(probs[:, i : i + HEAD] for i in range(0, KEYS, HEAD))
        add = jnp.dot(probs.astype(BF), s.vg[u], preferred_element_type=F32)
        s.acc[rows, :HEAD] = s.acc[rows, :HEAD] * shrink + add
        s.acc[rows, HEAD:] = s.acc[rows, HEAD:] * shrink + lanes
        s.peak[rows] = new

    prepare(z)
    here = pl.ds(pl.multiple_of(z * TALL, TALL), TALL)
    pos = s.pos[...].astype(F32) - (place.me * KEYS).astype(F32)
    update(here, mine, jnp.concatenate([upright(pos)] * HEADS, axis=0))
    for k in (1, 2, 3):

        @pl.when(z + k <= 3)
        def _(k=k):
            landed(s.qg.at[ups[k]], s.q_recv.at[ups[k]], place)
            prepare(ups[k])

    def arrivals(n):
        if n == 1:
            got_k(other[0])
            got_v(other[0])
        elif n == 2:
            aside()
            got_k(own[3])
            send(s.kg, s.k_recv, own[3], place.right, place.sib)
            got_k(own[1])
            send(s.kg, s.k_recv, own[1], place.sib)
            got_v(own[1])
            send(s.vg, s.v_recv, own[1], place.left, place.sib)
            got_v(own[3])
            send(s.vg, s.v_recv, own[3], place.sib)
        elif n == 4:
            got_k(other[3])
            got_v(other[3])
        elif n == 5:
            got_k(other[1])
            got_v(other[1])
        elif n == 6:
            got_k(own[2])
            send(s.kg, s.k_recv, own[2], place.sib)
            got_v(own[2])
            send(s.vg, s.v_recv, own[2], place.sib)
        elif n == 7:
            got_k(other[2])
            got_v(other[2])

    def step(i, carry):
        for n in (1, 2, 4, 5, 6, 7):

            @pl.when(i == n)
            def _(n=n):
                arrivals(n)

        u = order[0]
        for n in range(1, 8):
            u = jnp.where(i == n, order[n], u)
        first = z + (u >= mine).astype(jnp.int32)
        for n in range(4):

            @pl.when(first == n)
            def _(n=n):
                update(slice(n * TALL, 4 * TALL), u)

        return carry

    lax.fori_loop(0, 8, step, 0)

    eye_r = lax.broadcasted_iota(jnp.int32, (HEAD, HEAD), 0)
    eye_c = lax.broadcasted_iota(jnp.int32, (HEAD, HEAD), 1)
    eye = eye_r == eye_c

    def back(zq):
        def one(src, dst, send, recv):
            return pltpu.make_async_remote_copy(
                src_ref=src.at[zq],
                dst_ref=dst.at[z],
                send_sem=send.at[zq],
                recv_sem=recv.at[z],
                device_id={"ctx": place.spot(zq, place.x, a)},
                device_id_type=MESH,
            )

        return (
            one(s.o_out, s.o_in, s.o_send, s.o_recv),
            one(s.l_out, s.l_in, s.l_send, s.l_recv),
        )

    def finish(i, carry):
        zq = 3 - i
        rows = pl.ds(pl.multiple_of(zq * TALL, TALL), TALL)
        total = jnp.sum(s.acc[rows, HEAD:], axis=1, keepdims=True)
        s.o_out[zq] = (s.acc[rows, :HEAD] / total).astype(BF)
        level = s.peak[rows] * SCALE + jnp.log2(total)
        for half in range(2):
            block = level[half * HEAD : (half + 1) * HEAD]
            s.l_out[zq, half : half + 1, :] = jnp.sum(
                jnp.where(eye, block, 0.0), axis=0, keepdims=True
            )
        for copy in back(zq):
            copy.start()
        return carry

    lax.fori_loop(0, 3 - z, finish, 0)

    s.level[...] = s.peak[here] * SCALE
    s.mix[...] = s.acc[here, :HEAD]
    s.mass[...] = jnp.sum(s.acc[here, HEAD:], axis=1, keepdims=True) + jnp.zeros((TALL, HEAD), F32)
    for k in (1, 2, 3):

        @pl.when(z >= k)
        def _(k=k):
            zs = z - k
            landed(s.o_in.at[zs], s.o_recv.at[zs], place)
            landed(s.l_in.at[zs], s.l_recv.at[zs], place)
            spread = []
            for half in range(2):
                line = s.l_in[zs, half : half + 1, :]
                spread.append(jnp.sum(jnp.where(eye, line, 0.0), axis=1, keepdims=True))
            level = jnp.concatenate(spread, axis=0) + jnp.zeros((TALL, HEAD), F32)
            old = s.level[...]
            new = jnp.maximum(old, level)
            shrink, weight = jnp.exp2(old - new), jnp.exp2(level - new)
            s.mix[...] = s.mix[...] * shrink + weight * s.o_in[zs].astype(F32)
            s.mass[...] = s.mass[...] * shrink + weight
            s.level[...] = new

    def settle():
        for k in (1, 2, 3):

            @pl.when(z >= k)
            def _(k=k):
                q_copy(k).wait_send()

        def last(i, carry):
            for copy in back(3 - i):
                copy.wait_send()
            return carry

        lax.fori_loop(0, 3 - z, last, 0)
        mail.drain()

    return s.mix[...] / s.mass[...], settle


ATTEND_SCRATCH = dict(
    kg=pltpu.VMEM((8, KEYS, HEAD), BF),
    vg=pltpu.VMEM((8, KEYS, HEAD), BF),
    qg=pltpu.VMEM((4, ROWS, HEADS * HEAD), BF),
    q2=pltpu.VMEM((4 * TALL, HEAD), BF),
    peak=pltpu.VMEM((4 * TALL, HEAD), F32),
    acc=pltpu.VMEM((4 * TALL, 2 * HEAD), F32),
    level=pltpu.VMEM((TALL, HEAD), F32),
    mix=pltpu.VMEM((TALL, HEAD), F32),
    mass=pltpu.VMEM((TALL, HEAD), F32),
    o_out=pltpu.VMEM((4, TALL, HEAD), BF),
    o_in=pltpu.VMEM((4, TALL, HEAD), BF),
    l_out=pltpu.VMEM((4, 8, HEAD), F32),
    l_in=pltpu.VMEM((4, 8, HEAD), F32),
    kv_send=pltpu.SemaphoreType.DMA((16,)),
    q_send=pltpu.SemaphoreType.DMA((4,)),
    q_recv=pltpu.SemaphoreType.DMA((4,)),
    k_recv=pltpu.SemaphoreType.DMA((8,)),
    v_recv=pltpu.SemaphoreType.DMA((8,)),
    o_send=pltpu.SemaphoreType.DMA((4,)),
    o_recv=pltpu.SemaphoreType.DMA((4,)),
    l_send=pltpu.SemaphoreType.DMA((4,)),
    l_recv=pltpu.SemaphoreType.DMA((4,)),
)


def steps(index, edges):
    return sum((index >= edge).astype(jnp.int32) for edge in edges)


def slot_columns(ids_ref, kept_ref):
    lane = lax.broadcasted_iota(jnp.int32, (ROWS, HEAD), 1)
    flags = []
    for k in range(2):
        ids = upright(ids_ref[k : k + 1, :].astype(F32))
        kept = upright(kept_ref[k : k + 1, :].astype(F32))
        flags.append(((ids == lane.astype(F32)) & (kept == 1.0)).astype(F32))
    before = (
        lax.broadcasted_iota(jnp.int32, (ROWS, ROWS), 1)
        < lax.broadcasted_iota(jnp.int32, (ROWS, ROWS), 0)
    ).astype(F32)
    columns = []
    passed = jnp.zeros((1, HEAD), F32)
    for flag in flags:
        rank = passed + jnp.dot(before, flag, preferred_element_type=F32)
        passed = passed + jnp.sum(flag, axis=0, keepdims=True)
        slot = flag * (lane.astype(F32) * SLOTS + rank + 1.0)
        columns.append(jnp.sum(slot, axis=1, keepdims=True) - 1.0)
    return columns


def slot_and_head(index):
    expert = steps(index, range(PIECE, EXPERTS * PIECE, PIECE))
    within = index - expert * PIECE
    head = steps(within, range(SLOTS, PIECE, SLOTS))
    return (expert * SLOTS + within - head * SLOTS).astype(F32), head


def pick_rows(columns):
    shape = (EXPERTS * PIECE, TALL)
    slot, head = slot_and_head(lax.broadcasted_iota(jnp.int32, shape, 0))
    lane = lax.broadcasted_iota(jnp.int32, (ROWS, TALL), 1)
    group = steps(lane, range(ROWS, TALL, ROWS))
    same = lax.broadcasted_iota(jnp.int32, (ROWS, TALL), 0) == lane - group * ROWS
    hit = jnp.zeros(shape, F32)
    for column in columns:
        line = jnp.sum(jnp.where(same, column, 0.0), axis=0, keepdims=True)
        hit = hit + (line == slot).astype(F32)
    lanes = lax.broadcasted_iota(jnp.int32, shape, 1)
    hit = jnp.where(steps(lanes, range(ROWS, TALL, ROWS)) == head, hit, 0.0)
    return hit.astype(BF)


def place_rows(column):
    shape = (TALL, EXPERTS * PIECE)
    slot, head = slot_and_head(lax.broadcasted_iota(jnp.int32, shape, 1))
    tall = jnp.concatenate([column] * HEADS, axis=0)
    rows = lax.broadcasted_iota(jnp.int32, shape, 0)
    hit = (slot == tall) & (steps(rows, range(ROWS, TALL, ROWS)) == head)
    return hit.astype(F32).astype(BF)


def swap_matrix():
    side = 4 * PIECE
    row = lax.broadcasted_iota(jnp.int32, (side, side), 0)
    col = lax.broadcasted_iota(jnp.int32, (side, side), 1)
    first = steps(row, (PIECE, 2 * PIECE, 3 * PIECE))
    within = row - first * PIECE
    second = steps(within, (SLOTS, 2 * SLOTS, 3 * SLOTS))
    slot = within - second * SLOTS
    return (col == second * PIECE + first * SLOTS + slot).astype(F32).astype(BF)


def tables(s):
    columns = slot_columns(s.ids, s.kept)
    s.take[...] = pick_rows(columns)
    for k in range(2):
        s.spread[k] = place_rows(columns[k])
    s.swap[...] = swap_matrix()
    part = lax.broadcasted_iota(jnp.int32, (PIECE, HEAD), 0)
    part = steps(part, (SLOTS, 2 * SLOTS, 3 * SLOTS))
    for f in range(EXPERTS):
        gain = s.gain_in[f * HEADS : f * HEADS + 1, :].astype(F32)
        for h in range(1, HEADS):
            at = f * HEADS + h
            gain = jnp.where(part >= h, s.gain_in[at : at + 1, :].astype(F32), gain)
        s.gain[f] = gain


def experts(place, hidden, weights, s):
    a, e = place.a, place.e
    mail = Mail(place, s.send)

    chosen = jnp.dot(s.take[...], hidden, preferred_element_type=F32).astype(BF)
    for j in range(EXPERTS):
        s.pick[j] = chosen[j * PIECE : (j + 1) * PIECE]
    for j in range(1, EXPERTS):
        to = place.ek[j]
        mail.ship(s.pick, to, s.picked, e, s.picked_recv, e, exp=to)
    s.picked[e] = s.pick[e]
    ring = lax.broadcasted_iota(jnp.int32, (PIECE, PIECE), 0)
    ring = ring - SLOTS * steps(ring, (SLOTS, 2 * SLOTS, 3 * SLOTS))
    lap = lax.broadcasted_iota(jnp.int32, (PIECE, PIECE), 1)
    lap = lap - SLOTS * steps(lap, (SLOTS, 2 * SLOTS, 3 * SLOTS))
    alike = (ring == lap).astype(F32)
    for j in range(1, EXPERTS):
        f = place.ek[j]
        landed(s.picked.at[f], s.picked_recv.at[f], place)

    squares = jnp.zeros((PIECE, HEAD), F32)
    for f in range(EXPERTS):
        x = s.picked[f].astype(F32)
        squares = squares + x * x
    squares = jnp.sum(squares, axis=1, keepdims=True) + jnp.zeros((PIECE, HEAD), F32)
    total = jnp.dot(alike, squares, precision=lax.Precision.HIGHEST, preferred_element_type=F32)
    scale = lax.rsqrt(total / MODEL + EPS)
    me = place.me
    for f in range(EXPERTS):
        s.rows[me, :, f * HEAD : (f + 1) * HEAD] = (
            s.picked[f].astype(F32) * scale * s.gain[f]
        ).astype(BF)

    def forward(slot, *targets):
        for target in targets:
            mail.ship(s.rows, slot, s.rows, slot, s.rows_recv, slot, ctx=target)

    def got(k, r, core):
        slot = place.piece(k, r, core)
        landed(s.rows.at[slot], s.rows_recv.at[slot], place)
        return slot

    forward(me, place.column(2), place.column(1))

    def fan(k):
        slot = me if k == 0 else got(k, 0, a)
        if k == 2:
            forward(slot, place.column(1))
        forward(slot, place.right, place.left)
        if k >= 2:
            forward(slot, place.far)
        forward(slot, place.sib)

    def relay(k):
        slot = got(k, 3, a)
        if k == 0:
            forward(slot, place.right)
        forward(slot, place.sib)
        slot = got(k, 1, a)
        if k == 1:
            forward(slot, place.left)
        forward(slot, place.sib)

    def end(k):
        forward(got(k, 2, a), place.sib)

    def gather_siblings(k):
        for r in range(4):
            got(k, r, 1 - a)

    def groups(k):
        return [[(r, core) for r in pair_of for core in range(2)] for pair_of in ((2, 1), (3, 0))]

    def arrange(ks):
        for m, k in enumerate(ks):
            for n, group in enumerate(groups(k)):
                slots = [place.piece(k, r, core) for r, core in group]
                stack = jnp.concatenate([s.rows[slot] for slot in slots], axis=0)
                turned = jnp.dot(s.swap[...], stack, preferred_element_type=F32).astype(BF)
                top = (2 * m + n) * PIECE
                for h in range(HEADS):
                    for f in range(EXPERTS):
                        at = (f * HEADS + h) * HEAD
                        s.x[top : top + PIECE, at : at + HEAD] = turned[
                            h * PIECE : (h + 1) * PIECE, f * HEAD : (f + 1) * HEAD
                        ]

    def middle(task):
        s.g[...] = lax.dot_general(s.x[...], s.w_gate[...], NT, preferred_element_type=F32)
        task()
        u = lax.dot_general(s.x[...], s.w_up[...], NT, preferred_element_type=F32)
        g = s.g[...]
        s.act[...] = (g / (1.0 + jnp.exp(-g)) * u).astype(BF)

    def down(task):
        for at in range(0, MODEL, 1024):
            cols = slice(at, at + 1024)
            s.y[:, cols] = jnp.dot(s.act[...], s.w_down[:, cols], preferred_element_type=F32).astype(BF)
            if at == 1024:
                task()

    def hand_over(m, k):
        for n, group in enumerate(groups(k)):
            top = (2 * m + n) * PIECE
            tall = []
            for h in range(HEADS):
                at = [(f * HEADS + h) * HEAD for f in range(EXPERTS)]
                tall.append(
                    jnp.concatenate([s.y[top : top + PIECE, i : i + HEAD] for i in at], axis=1)
                )
            stack = jnp.concatenate(tall, axis=0)
            turned = jnp.dot(s.swap[...], stack, preferred_element_type=F32).astype(BF)
            for p, (r, core) in enumerate(group):
                s.sums[place.piece(k, r, core)] = turned[p * PIECE : (p + 1) * PIECE]
            for r in dict.fromkeys(r for r, _ in group):
                slot, to = place.piece(k, r, 1 - a), k * 4 + r
                mail.ship(s.sums, slot, s.beside, to, s.beside_recv, to, ctx=place.sib)

    def pair(k, r, *more):
        n = k * 4 + r
        landed(s.beside.at[n], s.beside_recv.at[n], place)
        total = s.sums[place.piece(k, r, a)].astype(F32) + s.beside[n].astype(F32)
        for ref, recv in more:
            landed(ref, recv, place)
            total = total + ref[...].astype(F32)
        slot = place.piece(k, r, a)
        s.sums[slot] = total.astype(BF)
        return slot

    def reduce_far(k):
        target = place.right if k % 2 == 0 else place.left
        mail.ship(s.sums, pair(k, 2), s.relayed, k, s.relayed_recv, k, ctx=target)

    def reduce_near(k, joined):
        r = 1 if (k % 2 == 0) == joined else 3
        more = ((s.relayed.at[k], s.relayed_recv.at[k]),) if joined else ()
        src = pair(k, r, *more)
        if r == 1:
            mail.ship(s.sums, src, s.from_left, k, s.left_recv, k, ctx=place.right)
        else:
            mail.ship(s.sums, src, s.from_right, k, s.right_recv, k, ctx=place.left)

    def reduce_own(k, *more):
        sides = ((s.from_left.at[k], s.left_recv.at[k]), (s.from_right.at[k], s.right_recv.at[k]))
        src = pair(k, 0, *sides, *more)
        if k > 0:
            mail.ship(s.sums, src, s.from_z, k, s.z_recv, k, ctx=place.column(k))

    def z_in(k):
        return (s.from_z.at[k], s.z_recv.at[k])

    def work(ks, *tasks):
        for k in ks:
            gather_siblings(k)
        arrange(ks)
        if ks[0] == 0:
            for copy in weights:
                copy.wait()
        middle(tasks[0])
        tasks[1]()
        down(tasks[2])
        for m, k in reversed(list(enumerate(ks))):
            hand_over(m, k)

    def send_first(*ks):
        for k in ks:
            reduce_far(k)
        for k in ks:
            reduce_near(k, False)

    fan(0)
    fan(1)
    relay(0)
    fan(2)
    relay(1)
    fan(3)
    end(0)
    end(1)
    work((0, 1), lambda: relay(2), lambda: relay(3), lambda: end(2))
    end(3)
    send_first(1, 0)
    work((2, 3), lambda: reduce_near(1, True), lambda: reduce_near(0, True), lambda: reduce_own(1))
    send_first(3, 2)
    reduce_own(0)
    reduce_near(3, True)
    reduce_near(2, True)
    reduce_own(3)
    reduce_own(2)
    total = s.sums[me].astype(F32)
    for k in (1, 2, 3):
        landed(*z_in(k), place)
        total = total + s.from_z[k].astype(F32)
    total = total.astype(BF)
    for f in range(EXPERTS):
        s.done[f] = total[:, f * HEAD : (f + 1) * HEAD]
    for j in range(1, EXPERTS):
        to = place.ek[j]
        mail.ship(s.done, to, s.home, e, s.home_recv, e, exp=to)
    s.home[e] = s.done[e]
    for j in range(1, EXPERTS):
        f = place.ek[j]
        landed(s.home.at[f], s.home_recv.at[f], place)
    back = jnp.concatenate([s.home[j] for j in range(EXPERTS)], axis=0)
    mixed = jnp.zeros((TALL, HEAD), F32)
    for k in range(2):
        gate = jnp.concatenate([upright(s.gates[k : k + 1, :])] * HEADS, axis=0)
        mixed = mixed + gate * jnp.dot(s.spread[k], back, preferred_element_type=F32)
    return mixed, mail.drain


def piece_buffers(count):
    return pltpu.VMEM((count, PIECE, WIDE), BF)


EXPERT_SCRATCH = dict(
    w_gate=pltpu.VMEM((HIDDEN, MODEL), BF),
    w_up=pltpu.VMEM((HIDDEN, MODEL), BF),
    w_down=pltpu.VMEM((HIDDEN, MODEL), BF),
    take=pltpu.VMEM((EXPERTS * PIECE, TALL), BF),
    swap=pltpu.VMEM((4 * PIECE, 4 * PIECE), BF),
    gain=pltpu.VMEM((EXPERTS, PIECE, HEAD), F32),
    pick=pltpu.VMEM((EXPERTS, PIECE, HEAD), BF),
    picked=pltpu.VMEM((EXPERTS, PIECE, HEAD), BF),
    spread=pltpu.VMEM((2, TALL, EXPERTS * PIECE), BF),
    rows=piece_buffers(32),
    x=pltpu.VMEM((4 * PIECE, MODEL), BF),
    g=pltpu.VMEM((4 * PIECE, HIDDEN), F32),
    act=pltpu.VMEM((4 * PIECE, HIDDEN), BF),
    y=pltpu.VMEM((4 * PIECE, MODEL), BF),
    sums=piece_buffers(32),
    beside=piece_buffers(16),
    relayed=piece_buffers(4),
    from_left=piece_buffers(4),
    from_right=piece_buffers(4),
    from_z=piece_buffers(4),
    done=pltpu.VMEM((EXPERTS, PIECE, HEAD), BF),
    home=pltpu.VMEM((EXPERTS, PIECE, HEAD), BF),
    send=pltpu.SemaphoreType.DMA((80,)),
    picked_recv=pltpu.SemaphoreType.DMA((EXPERTS,)),
    rows_recv=pltpu.SemaphoreType.DMA((32,)),
    beside_recv=pltpu.SemaphoreType.DMA((16,)),
    relayed_recv=pltpu.SemaphoreType.DMA((4,)),
    left_recv=pltpu.SemaphoreType.DMA((4,)),
    right_recv=pltpu.SemaphoreType.DMA((4,)),
    z_recv=pltpu.SemaphoreType.DMA((4,)),
    home_recv=pltpu.SemaphoreType.DMA((EXPERTS,)),
)


LOCAL_SCRATCH = dict(
    res=pltpu.VMEM((ROWS, HEADS * HEAD), BF),
    hidden=pltpu.VMEM((TALL, HEAD), BF),
    pos=pltpu.VMEM((1, ROWS), jnp.int32),
    gain_in=pltpu.VMEM((32, HEAD), BF),
    ids=pltpu.VMEM((2, ROWS), jnp.int32),
    kept=pltpu.VMEM((2, ROWS), jnp.int32),
    gates=pltpu.VMEM((2, ROWS), F32),
    local_sem=pltpu.SemaphoreType.DMA((12,)),
)
SCRATCH = ATTEND_SCRATCH | EXPERT_SCRATCH | LOCAL_SCRATCH


def layer_kernel(res, q, key, value, pos, gain, wg, wu, wd, ids, kept, gates, out_ref, *scratch):
    s = types.SimpleNamespace(**dict(zip(SCRATCH, scratch)))
    place = Place()
    mine = place.x * 2 + place.a
    moves = dict(
        k=(key, s.kg.at[mine]),
        v=(value, s.vg.at[mine]),
        q=(q, s.qg.at[place.z]),
        pos=(pos, s.pos),
        ids=(ids, s.ids),
        kept=(kept, s.kept),
        gates=(gates, s.gates),
        gain=(gain, s.gain_in),
        res=(res, s.res),
        wg=(wg.at[0], s.w_gate),
        wu=(wu.at[0], s.w_up),
        wd=(wd.at[0], s.w_down),
    )
    local = {
        name: pltpu.make_async_copy(src, dst, s.local_sem.at[i])
        for i, (name, (src, dst)) in enumerate(moves.items())
    }
    for copy in local.values():
        copy.start()
    greet(place)

    for name in ("pos",):
        local[name].wait()

    def aside():
        for name in ("ids", "kept", "gates", "gain", "res"):
            local[name].wait()
        tables(s)

    attended, settle = attention(place, s, local, aside)
    tall = []
    for h in range(HEADS):
        res_h = s.res[:, h * HEAD : (h + 1) * HEAD].astype(F32)
        tall.append((res_h + attended[h * ROWS : (h + 1) * ROWS]).astype(BF))
    hidden = jnp.concatenate(tall, axis=0)
    s.hidden[...] = hidden
    weights = [local[name] for name in ("wg", "wu", "wd")]
    mixed, drain = experts(place, hidden, weights, s)
    for h in range(HEADS):
        rows = slice(h * ROWS, (h + 1) * ROWS)
        out_ref[:, h * HEAD : (h + 1) * HEAD] = (s.hidden[rows].astype(F32) + mixed[rows]).astype(BF)
    settle()
    drain()


def body(
    residual_in,
    queries,
    context_key_cache,
    context_value_cache,
    query_pos,
    norm_gain,
    w_gate,
    w_up,
    w_down,
    expert_ids,
    kept_choices,
    gate_weights,
):
    any_spec = pl.BlockSpec(memory_space=pl.ANY)
    return pl.pallas_call(
        layer_kernel,
        out_shape=jax.ShapeDtypeStruct((ROWS, HEADS * HEAD), BF),
        in_specs=[any_spec] * 12,
        out_specs=pl.BlockSpec(memory_space=pltpu.VMEM),
        scratch_shapes=list(SCRATCH.values()),
        compiler_params=pltpu.CompilerParams(
            collective_id=0, has_side_effects=True, vmem_limit_bytes=56 * 2**20
        ),
        name="layer",
    )(
        residual_in,
        queries,
        context_key_cache,
        context_value_cache,
        query_pos.reshape(1, ROWS),
        norm_gain.reshape(32, HEAD),
        w_gate,
        w_up,
        w_down,
        expert_ids.T,
        kept_choices.T,
        gate_weights.T,
    )


def solution(mesh):
    in_specs = (
        P("ctx", "exp"),
        P("ctx", "exp"),
        P("ctx", "exp"),
        P("ctx", "exp"),
        P("ctx"),
        P(),
        P("exp", "ctx", None),
        P("exp", "ctx", None),
        P("exp", "ctx", None),
        P("ctx", None),
        P("ctx", None),
        P("ctx", None),
    )
    out_specs = P("ctx", "exp")
    return jax.shard_map(body, mesh=mesh, in_specs=in_specs, out_specs=out_specs, check_vma=False)
```

```python
import math
import types

import jax
import jax.numpy as jnp
from jax import lax
from jax.experimental import pallas as pl
from jax.experimental.pallas import tpu as pltpu
from jax.sharding import PartitionSpec as P

BF = jnp.bfloat16
F32 = jnp.float32
MESH = pl.DeviceIdType.MESH
NT = (((1,), (1,)), ((), ()))
NN = (((1,), (0,)), ((), ()))
HEAD = 128
ROWS = 64
HEADS = 4
TALL = ROWS * HEADS
KEYS = 1024
MODEL = 4096
HIDDEN = 448
EXPERTS = 8
SLOTS = 12
PIECE = SLOTS * HEADS
WIDE = EXPERTS * HEAD
NEG = -1e30
EPS = 1e-05
DIRECT = (2, 3)
SCALE = HEAD ** (-0.5) * math.log2(math.e)


class Place:
    def __init__(self):
        self.me = lax.axis_index("ctx")
        self.e = lax.axis_index("exp")
        self.z = lax.div(self.me, 8)
        self.x = lax.rem(lax.div(self.me, 2), 4)
        self.a = lax.rem(self.me, 2)
        z = self.z
        self.zk = [z, z + 1 - 2 * lax.rem(z, 2), z + 2 - 4 * lax.div(z, 2), 3 - z]
        self.xr = [self.x] + [lax.rem(self.x + r, 4) for r in (1, 2, 3)]
        self.sib = self.spot(self.z, self.x, 1 - self.a)
        self.right = self.spot(self.z, self.xr[1], self.a)
        self.left = self.spot(self.z, self.xr[3], self.a)
        self.far = self.spot(self.z, self.xr[2], self.a)
        self.ek = [lax.rem(self.e + j, EXPERTS) for j in range(EXPERTS)]

    def spot(self, z, x, a):
        return z * 8 + x * 2 + a

    def piece(self, k, r, a):
        return self.spot(self.zk[k], self.xr[r], a)

    def column(self, k):
        return self.spot(self.zk[k], self.x, self.a)


class Mail:
    def __init__(self, place, sems):
        self.place, self.sems, self.used, self.open = place, sems, 0, []

    def ship(self, ref, at, to_ref, to, recv, recv_at, ctx=None, exp=None):
        target = {name: to_ for name, to_ in (("ctx", ctx), ("exp", exp)) if to_ is not None}
        number = self.used
        self.used += 1

        def make():
            return pltpu.make_async_remote_copy(
                src_ref=ref.at[at],
                dst_ref=to_ref.at[to],
                send_sem=self.sems.at[number],
                recv_sem=recv.at[recv_at],
                device_id=target,
                device_id_type=MESH,
            )

        make().start()
        self.open.append(make)

    def drain(self):
        for make in self.open:
            make().wait_send()
        self.open = []


def landed(slot, recv_sem, place):
    pltpu.make_async_remote_copy(
        src_ref=slot,
        dst_ref=slot,
        send_sem=recv_sem,
        recv_sem=recv_sem,
        device_id={"ctx": place.sib},
        device_id_type=MESH,
    ).wait_recv()


def wide(x, times):
    return jnp.concatenate([x] * times, axis=1)


def upright(line):
    row = lax.broadcasted_iota(jnp.int32, (ROWS, ROWS), 0)
    col = lax.broadcasted_iota(jnp.int32, (ROWS, ROWS), 1)
    return jnp.sum(jnp.where(row == col, line, 0.0), axis=1, keepdims=True)


def greet(place):
    barrier = pltpu.get_barrier_semaphore()
    peers = [{"ctx": c} for c in (place.sib, place.right, place.left, place.far)]
    peers += [
        {"ctx": place.column(k), "exp": place.ek[j]}
        for k in range(4)
        for j in range(EXPERTS)
        if k or j
    ]
    for peer in peers:
        pl.semaphore_signal(barrier, inc=1, device_id=peer, device_id_type=MESH)
    pl.semaphore_wait(barrier, len(peers))


def attention(place, s, local, aside):
    z, a = place.z, place.a
    mail = Mail(place, s.kv_send)
    units = [[x * 2, x * 2 + 1] for x in place.xr]
    own = [lax.select(a == 0, u[0], u[1]) for u in units]
    other = [lax.select(a == 0, u[1], u[0]) for u in units]
    mine = own[0]
    order = [own[0], other[0], own[3], own[1], other[3], other[1], own[2], other[2]]

    downs = [place.spot(z - k, place.x, a) for k in range(4)]
    ups = [z + k for k in range(4)]

    def q_copy(k):
        return pltpu.make_async_remote_copy(
            src_ref=s.qg.at[z],
            dst_ref=s.qg.at[z],
            send_sem=s.q_send.at[k],
            recv_sem=s.q_recv.at[z],
            device_id={"ctx": downs[k]},
            device_id_type=MESH,
        )

    def send(ref, sem, u, *targets):
        for target in targets:
            mail.ship(ref, u, ref, u, sem, u, ctx=target)

    def got_k(u):
        landed(s.kg.at[u], s.k_recv.at[u], place)

    def got_v(u):
        landed(s.vg.at[u], s.v_recv.at[u], place)

    local["k"].wait()
    send(s.kg, s.k_recv, mine, place.right, place.left, place.sib)
    local["q"].wait()
    for k in (1, 2, 3):

        @pl.when(z >= k)
        def _(k=k):
            q_copy(k).start()

    local["v"].wait()
    send(s.vg, s.v_recv, mine, place.right, place.left, place.sib)

    s.peak[...] = jnp.full((4 * TALL, HEAD), NEG, F32)
    s.acc[...] = jnp.zeros((4 * TALL, 2 * HEAD), F32)

    def prepare(zq):
        for h in range(HEADS):
            at = pl.ds(pl.multiple_of(zq * TALL + h * ROWS, ROWS), ROWS)
            s.q2[at, :] = s.qg[zq, :, h * HEAD : (h + 1) * HEAD]

    def update(rows, u, pos_col=None):
        scores = lax.dot_general(s.q2[rows], s.kg[u], NT, preferred_element_type=F32)
        if pos_col is not None:
            key = lax.broadcasted_iota(jnp.int32, (TALL, KEYS), 1).astype(F32)
            scores = jnp.where(key <= pos_col, scores, NEG)
        old = s.peak[rows]
        new = jnp.maximum(old, jnp.max(scores, axis=1, keepdims=True))
        probs = jnp.exp2((scores - wide(new, KEYS // HEAD)) * SCALE)
        shrink = jnp.exp2((old - new) * SCALE)
        lanes = sum(probs[:, i : i + HEAD] for i in range(0, KEYS, HEAD))
        add = jnp.dot(probs.astype(BF), s.vg[u], preferred_element_type=F32)
        s.acc[rows, :HEAD] = s.acc[rows, :HEAD] * shrink + add
        s.acc[rows, HEAD:] = s.acc[rows, HEAD:] * shrink + lanes
        s.peak[rows] = new

    prepare(z)
    here = pl.ds(pl.multiple_of(z * TALL, TALL), TALL)
    pos = s.pos[...].astype(F32) - (place.me * KEYS).astype(F32)
    update(here, mine, jnp.concatenate([upright(pos)] * HEADS, axis=0))
    for k in (1, 2, 3):

        @pl.when(z + k <= 3)
        def _(k=k):
            landed(s.qg.at[ups[k]], s.q_recv.at[ups[k]], place)
            prepare(ups[k])

    def arrivals(n):
        if n == 1:
            got_k(other[0])
            got_v(other[0])
        elif n == 2:
            aside()
            got_k(own[3])
            send(s.kg, s.k_recv, own[3], place.right, place.sib)
            got_k(own[1])
            send(s.kg, s.k_recv, own[1], place.sib)
            got_v(own[1])
            send(s.vg, s.v_recv, own[1], place.left, place.sib)
            got_v(own[3])
            send(s.vg, s.v_recv, own[3], place.sib)
        elif n == 4:
            got_k(other[3])
            got_v(other[3])
        elif n == 5:
            got_k(other[1])
            got_v(other[1])
        elif n == 6:
            got_k(own[2])
            send(s.kg, s.k_recv, own[2], place.sib)
            got_v(own[2])
            send(s.vg, s.v_recv, own[2], place.sib)
        elif n == 7:
            got_k(other[2])
            got_v(other[2])

    def step(i, carry):
        for n in (1, 2, 4, 5, 6, 7):

            @pl.when(i == n)
            def _(n=n):
                arrivals(n)

        u = order[0]
        for n in range(1, 8):
            u = jnp.where(i == n, order[n], u)
        first = z + (u >= mine).astype(jnp.int32)
        for n in range(4):

            @pl.when(first == n)
            def _(n=n):
                update(slice(n * TALL, 4 * TALL), u)

        return carry

    lax.fori_loop(0, 8, step, 0)

    eye_r = lax.broadcasted_iota(jnp.int32, (HEAD, HEAD), 0)
    eye_c = lax.broadcasted_iota(jnp.int32, (HEAD, HEAD), 1)
    eye = eye_r == eye_c

    def back(zq):
        def one(src, dst, send, recv):
            return pltpu.make_async_remote_copy(
                src_ref=src.at[zq],
                dst_ref=dst.at[z],
                send_sem=send.at[zq],
                recv_sem=recv.at[z],
                device_id={"ctx": place.spot(zq, place.x, a)},
                device_id_type=MESH,
            )

        return (
            one(s.o_out, s.o_in, s.o_send, s.o_recv),
            one(s.l_out, s.l_in, s.l_send, s.l_recv),
        )

    def finish(i, carry):
        zq = 3 - i
        rows = pl.ds(pl.multiple_of(zq * TALL, TALL), TALL)
        total = jnp.sum(s.acc[rows, HEAD:], axis=1, keepdims=True)
        s.o_out[zq] = (s.acc[rows, :HEAD] / total).astype(BF)
        level = s.peak[rows] * SCALE + jnp.log2(total)
        for half in range(2):
            block = level[half * HEAD : (half + 1) * HEAD]
            s.l_out[zq, half : half + 1, :] = jnp.sum(
                jnp.where(eye, block, 0.0), axis=0, keepdims=True
            )
        for copy in back(zq):
            copy.start()
        return carry

    lax.fori_loop(0, 3 - z, finish, 0)

    s.level[...] = s.peak[here] * SCALE
    s.mix[...] = s.acc[here, :HEAD]
    s.mass[...] = jnp.sum(s.acc[here, HEAD:], axis=1, keepdims=True) + jnp.zeros((TALL, HEAD), F32)
    for k in (1, 2, 3):

        @pl.when(z >= k)
        def _(k=k):
            zs = z - k
            landed(s.o_in.at[zs], s.o_recv.at[zs], place)
            landed(s.l_in.at[zs], s.l_recv.at[zs], place)
            spread = []
            for half in range(2):
                line = s.l_in[zs, half : half + 1, :]
                spread.append(jnp.sum(jnp.where(eye, line, 0.0), axis=1, keepdims=True))
            level = jnp.concatenate(spread, axis=0) + jnp.zeros((TALL, HEAD), F32)
            old = s.level[...]
            new = jnp.maximum(old, level)
            shrink, weight = jnp.exp2(old - new), jnp.exp2(level - new)
            s.mix[...] = s.mix[...] * shrink + weight * s.o_in[zs].astype(F32)
            s.mass[...] = s.mass[...] * shrink + weight
            s.level[...] = new

    def settle():
        for k in (1, 2, 3):

            @pl.when(z >= k)
            def _(k=k):
                q_copy(k).wait_send()

        def last(i, carry):
            for copy in back(3 - i):
                copy.wait_send()
            return carry

        lax.fori_loop(0, 3 - z, last, 0)
        mail.drain()

    return s.mix[...] / s.mass[...], settle


ATTEND_SCRATCH = dict(
    kg=pltpu.VMEM((8, KEYS, HEAD), BF),
    vg=pltpu.VMEM((8, KEYS, HEAD), BF),
    qg=pltpu.VMEM((4, ROWS, HEADS * HEAD), BF),
    q2=pltpu.VMEM((4 * TALL, HEAD), BF),
    peak=pltpu.VMEM((4 * TALL, HEAD), F32),
    acc=pltpu.VMEM((4 * TALL, 2 * HEAD), F32),
    level=pltpu.VMEM((TALL, HEAD), F32),
    mix=pltpu.VMEM((TALL, HEAD), F32),
    mass=pltpu.VMEM((TALL, HEAD), F32),
    o_out=pltpu.VMEM((4, TALL, HEAD), BF),
    o_in=pltpu.VMEM((4, TALL, HEAD), BF),
    l_out=pltpu.VMEM((4, 8, HEAD), F32),
    l_in=pltpu.VMEM((4, 8, HEAD), F32),
    kv_send=pltpu.SemaphoreType.DMA((16,)),
    q_send=pltpu.SemaphoreType.DMA((4,)),
    q_recv=pltpu.SemaphoreType.DMA((4,)),
    k_recv=pltpu.SemaphoreType.DMA((8,)),
    v_recv=pltpu.SemaphoreType.DMA((8,)),
    o_send=pltpu.SemaphoreType.DMA((4,)),
    o_recv=pltpu.SemaphoreType.DMA((4,)),
    l_send=pltpu.SemaphoreType.DMA((4,)),
    l_recv=pltpu.SemaphoreType.DMA((4,)),
)


def steps(index, edges):
    return sum((index >= edge).astype(jnp.int32) for edge in edges)


def slot_columns(ids_ref, kept_ref):
    lane = lax.broadcasted_iota(jnp.int32, (ROWS, HEAD), 1)
    flags = []
    for k in range(2):
        ids = upright(ids_ref[k : k + 1, :].astype(F32))
        kept = upright(kept_ref[k : k + 1, :].astype(F32))
        flags.append(((ids == lane.astype(F32)) & (kept == 1.0)).astype(F32))
    before = (
        lax.broadcasted_iota(jnp.int32, (ROWS, ROWS), 1)
        < lax.broadcasted_iota(jnp.int32, (ROWS, ROWS), 0)
    ).astype(F32)
    columns = []
    passed = jnp.zeros((1, HEAD), F32)
    for flag in flags:
        rank = passed + jnp.dot(before, flag, preferred_element_type=F32)
        passed = passed + jnp.sum(flag, axis=0, keepdims=True)
        slot = flag * (lane.astype(F32) * SLOTS + rank + 1.0)
        columns.append(jnp.sum(slot, axis=1, keepdims=True) - 1.0)
    return columns


def slot_and_head(index):
    expert = steps(index, range(PIECE, EXPERTS * PIECE, PIECE))
    within = index - expert * PIECE
    head = steps(within, range(SLOTS, PIECE, SLOTS))
    return (expert * SLOTS + within - head * SLOTS).astype(F32), head


def pick_rows(columns):
    shape = (EXPERTS * PIECE, TALL)
    slot, head = slot_and_head(lax.broadcasted_iota(jnp.int32, shape, 0))
    lane = lax.broadcasted_iota(jnp.int32, (ROWS, TALL), 1)
    group = steps(lane, range(ROWS, TALL, ROWS))
    same = lax.broadcasted_iota(jnp.int32, (ROWS, TALL), 0) == lane - group * ROWS
    hit = jnp.zeros(shape, F32)
    for column in columns:
        line = jnp.sum(jnp.where(same, column, 0.0), axis=0, keepdims=True)
        hit = hit + (line == slot).astype(F32)
    lanes = lax.broadcasted_iota(jnp.int32, shape, 1)
    hit = jnp.where(steps(lanes, range(ROWS, TALL, ROWS)) == head, hit, 0.0)
    return hit.astype(BF)


def place_rows(column):
    shape = (TALL, EXPERTS * PIECE)
    slot, head = slot_and_head(lax.broadcasted_iota(jnp.int32, shape, 1))
    tall = jnp.concatenate([column] * HEADS, axis=0)
    rows = lax.broadcasted_iota(jnp.int32, shape, 0)
    hit = (slot == tall) & (steps(rows, range(ROWS, TALL, ROWS)) == head)
    return hit.astype(F32).astype(BF)


def swap_matrix():
    side = 4 * PIECE
    row = lax.broadcasted_iota(jnp.int32, (side, side), 0)
    col = lax.broadcasted_iota(jnp.int32, (side, side), 1)
    first = steps(row, (PIECE, 2 * PIECE, 3 * PIECE))
    within = row - first * PIECE
    second = steps(within, (SLOTS, 2 * SLOTS, 3 * SLOTS))
    slot = within - second * SLOTS
    return (col == second * PIECE + first * SLOTS + slot).astype(F32).astype(BF)


def tables(s):
    columns = slot_columns(s.ids, s.kept)
    s.take[...] = pick_rows(columns)
    for k in range(2):
        s.spread[k] = place_rows(columns[k])
    s.swap[...] = swap_matrix()
    part = lax.broadcasted_iota(jnp.int32, (PIECE, HEAD), 0)
    part = steps(part, (SLOTS, 2 * SLOTS, 3 * SLOTS))
    for f in range(EXPERTS):
        gain = s.gain_in[f * HEADS : f * HEADS + 1, :].astype(F32)
        for h in range(1, HEADS):
            at = f * HEADS + h
            gain = jnp.where(part >= h, s.gain_in[at : at + 1, :].astype(F32), gain)
        s.gain[f] = gain


def experts(place, hidden, weights, s):
    a, e = place.a, place.e
    mail = Mail(place, s.send)

    chosen = jnp.dot(s.take[...], hidden, preferred_element_type=F32).astype(BF)
    for j in range(EXPERTS):
        s.pick[j] = chosen[j * PIECE : (j + 1) * PIECE]
    for j in range(1, EXPERTS):
        to = place.ek[j]
        mail.ship(s.pick, to, s.picked, e, s.picked_recv, e, exp=to)
    s.picked[e] = s.pick[e]
    ring = lax.broadcasted_iota(jnp.int32, (PIECE, PIECE), 0)
    ring = ring - SLOTS * steps(ring, (SLOTS, 2 * SLOTS, 3 * SLOTS))
    lap = lax.broadcasted_iota(jnp.int32, (PIECE, PIECE), 1)
    lap = lap - SLOTS * steps(lap, (SLOTS, 2 * SLOTS, 3 * SLOTS))
    alike = (ring == lap).astype(F32)
    for j in range(1, EXPERTS):
        f = place.ek[j]
        landed(s.picked.at[f], s.picked_recv.at[f], place)

    squares = jnp.zeros((PIECE, HEAD), F32)
    for f in range(EXPERTS):
        x = s.picked[f].astype(F32)
        squares = squares + x * x
    squares = jnp.sum(squares, axis=1, keepdims=True) + jnp.zeros((PIECE, HEAD), F32)
    total = jnp.dot(alike, squares, precision=lax.Precision.HIGHEST, preferred_element_type=F32)
    scale = lax.rsqrt(total / MODEL + EPS)
    me = place.me
    for f in range(EXPERTS):
        s.rows[me, :, f * HEAD : (f + 1) * HEAD] = (
            s.picked[f].astype(F32) * scale * s.gain[f]
        ).astype(BF)

    def forward(slot, *targets):
        for target in targets:
            mail.ship(s.rows, slot, s.rows, slot, s.rows_recv, slot, ctx=target)

    def got(k, r, core):
        slot = place.piece(k, r, core)
        landed(s.rows.at[slot], s.rows_recv.at[slot], place)
        return slot

    forward(me, place.column(2), place.column(1))

    def fan(k):
        slot = me if k == 0 else got(k, 0, a)
        if k == 2:
            forward(slot, place.column(1))
        forward(slot, place.right, place.left)
        if k in DIRECT:
            forward(slot, place.far)
        forward(slot, place.sib)

    def relay(k):
        slot = got(k, 3, a)
        if k % 2 == 0 and k not in DIRECT:
            forward(slot, place.right)
        forward(slot, place.sib)
        slot = got(k, 1, a)
        if k % 2 == 1 and k not in DIRECT:
            forward(slot, place.left)
        forward(slot, place.sib)

    def end(k):
        forward(got(k, 2, a), place.sib)

    def gather_siblings(k):
        for r in range(4):
            got(k, r, 1 - a)

    def groups(k):
        return [[(r, core) for r in pair_of for core in range(2)] for pair_of in ((2, 1), (3, 0))]

    def arrange(ks):
        for m, k in enumerate(ks):
            for n, group in enumerate(groups(k)):
                slots = [place.piece(k, r, core) for r, core in group]
                stack = jnp.concatenate([s.rows[slot] for slot in slots], axis=0)
                turned = jnp.dot(s.swap[...], stack, preferred_element_type=F32).astype(BF)
                top = (2 * m + n) * PIECE
                for h in range(HEADS):
                    for f in range(EXPERTS):
                        at = (f * HEADS + h) * HEAD
                        s.x[top : top + PIECE, at : at + HEAD] = turned[
                            h * PIECE : (h + 1) * PIECE, f * HEAD : (f + 1) * HEAD
                        ]

    def middle(task):
        s.g[...] = lax.dot_general(s.x[...], s.w_gate[...], NT, preferred_element_type=F32)
        task()
        u = lax.dot_general(s.x[...], s.w_up[...], NT, preferred_element_type=F32)
        g = s.g[...]
        s.act[...] = (g / (1.0 + jnp.exp(-g)) * u).astype(BF)

    def down(task):
        for at in range(0, MODEL, 1024):
            cols = slice(at, at + 1024)
            s.y[:, cols] = jnp.dot(s.act[...], s.w_down[:, cols], preferred_element_type=F32).astype(BF)
            if at == 1024:
                task()

    def hand_over(m, k):
        for n, group in enumerate(groups(k)):
            top = (2 * m + n) * PIECE
            tall = []
            for h in range(HEADS):
                at = [(f * HEADS + h) * HEAD for f in range(EXPERTS)]
                tall.append(
                    jnp.concatenate([s.y[top : top + PIECE, i : i + HEAD] for i in at], axis=1)
                )
            stack = jnp.concatenate(tall, axis=0)
            turned = jnp.dot(s.swap[...], stack, preferred_element_type=F32).astype(BF)
            for p, (r, core) in enumerate(group):
                s.sums[place.piece(k, r, core)] = turned[p * PIECE : (p + 1) * PIECE]
            for r in dict.fromkeys(r for r, _ in group):
                slot, to = place.piece(k, r, 1 - a), k * 4 + r
                mail.ship(s.sums, slot, s.beside, to, s.beside_recv, to, ctx=place.sib)

    def pair(k, r, *more):
        n = k * 4 + r
        landed(s.beside.at[n], s.beside_recv.at[n], place)
        total = s.sums[place.piece(k, r, a)].astype(F32) + s.beside[n].astype(F32)
        for ref, recv in more:
            landed(ref, recv, place)
            total = total + ref[...].astype(F32)
        slot = place.piece(k, r, a)
        s.sums[slot] = total.astype(BF)
        return slot

    def reduce_far(k):
        target = place.right if k % 2 == 0 else place.left
        mail.ship(s.sums, pair(k, 2), s.relayed, k, s.relayed_recv, k, ctx=target)

    def reduce_near(k, joined):
        r = 1 if (k % 2 == 0) == joined else 3
        more = ((s.relayed.at[k], s.relayed_recv.at[k]),) if joined else ()
        src = pair(k, r, *more)
        if r == 1:
            mail.ship(s.sums, src, s.from_left, k, s.left_recv, k, ctx=place.right)
        else:
            mail.ship(s.sums, src, s.from_right, k, s.right_recv, k, ctx=place.left)

    def reduce_own(k):
        sides = ((s.from_left.at[k], s.left_recv.at[k]), (s.from_right.at[k], s.right_recv.at[k]))
        total = s.sums[pair(k, 0, *sides)]
        for f in range(EXPERTS):
            s.done[k, f] = total[:, f * HEAD : (f + 1) * HEAD]
        for j in reversed(range(EXPERTS)):
            to = place.ek[j]
            if k or j:
                where = dict(ctx=place.column(k), exp=to)
                mail.ship(s.done, (k, to), s.home, (k, e), s.home_recv, k * EXPERTS + e, **where)
            else:
                s.home[0, e] = s.done[0, e]

    def work(ks, *tasks):
        for k in ks:
            gather_siblings(k)
        arrange(ks)
        if ks[0] == 0:
            for copy in weights:
                copy.wait()
        middle(tasks[0])
        tasks[1]()
        down(tasks[2])
        for m, k in reversed(list(enumerate(ks))):
            hand_over(m, k)

    def send_first(*ks):
        for k in ks:
            reduce_far(k)
        for k in ks:
            reduce_near(k, False)

    def idle():
        return None

    fan(0)
    fan(1)
    relay(0)
    fan(2)
    relay(1)
    fan(3)
    end(0)
    end(1)
    relay(2)
    work((0, 1), lambda: relay(3), lambda: end(2), lambda: end(3))
    send_first(1, 0)
    work((2, 3), idle, idle, idle)
    send_first(3, 2)
    reduce_near(1, True)
    reduce_near(0, True)
    reduce_near(3, True)
    reduce_near(2, True)
    reduce_own(1)
    reduce_own(0)
    reduce_own(3)
    reduce_own(2)
    gates = [
        jnp.concatenate([upright(s.gates[k : k + 1, :])] * HEADS, axis=0) for k in range(2)
    ]
    for k in (1, 0, 3, 2):
        for j in range(EXPERTS):
            if k or j:
                f = place.ek[j]
                landed(s.home.at[k, f], s.home_recv.at[k * EXPERTS + f], place)
    back = jnp.concatenate(
        [sum(s.home[k, j].astype(F32) for k in range(4)).astype(BF) for j in range(EXPERTS)], axis=0
    )
    mixed = jnp.zeros((TALL, HEAD), F32)
    for k in range(2):
        mixed = mixed + gates[k] * jnp.dot(s.spread[k], back, preferred_element_type=F32)
    return mixed, mail.drain


def piece_buffers(count):
    return pltpu.VMEM((count, PIECE, WIDE), BF)


EXPERT_SCRATCH = dict(
    w_gate=pltpu.VMEM((HIDDEN, MODEL), BF),
    w_up=pltpu.VMEM((HIDDEN, MODEL), BF),
    w_down=pltpu.VMEM((HIDDEN, MODEL), BF),
    take=pltpu.VMEM((EXPERTS * PIECE, TALL), BF),
    swap=pltpu.VMEM((4 * PIECE, 4 * PIECE), BF),
    gain=pltpu.VMEM((EXPERTS, PIECE, HEAD), F32),
    pick=pltpu.VMEM((EXPERTS, PIECE, HEAD), BF),
    picked=pltpu.VMEM((EXPERTS, PIECE, HEAD), BF),
    spread=pltpu.VMEM((2, TALL, EXPERTS * PIECE), BF),
    rows=piece_buffers(32),
    x=pltpu.VMEM((4 * PIECE, MODEL), BF),
    g=pltpu.VMEM((4 * PIECE, HIDDEN), F32),
    act=pltpu.VMEM((4 * PIECE, HIDDEN), BF),
    y=pltpu.VMEM((4 * PIECE, MODEL), BF),
    sums=piece_buffers(32),
    beside=piece_buffers(16),
    relayed=piece_buffers(4),
    from_left=piece_buffers(4),
    from_right=piece_buffers(4),
    done=pltpu.VMEM((4, EXPERTS, PIECE, HEAD), BF),
    home=pltpu.VMEM((4, EXPERTS, PIECE, HEAD), BF),
    send=pltpu.SemaphoreType.DMA((112,)),
    picked_recv=pltpu.SemaphoreType.DMA((EXPERTS,)),
    rows_recv=pltpu.SemaphoreType.DMA((32,)),
    beside_recv=pltpu.SemaphoreType.DMA((16,)),
    relayed_recv=pltpu.SemaphoreType.DMA((4,)),
    left_recv=pltpu.SemaphoreType.DMA((4,)),
    right_recv=pltpu.SemaphoreType.DMA((4,)),
    home_recv=pltpu.SemaphoreType.DMA((4 * EXPERTS,)),
)


LOCAL_SCRATCH = dict(
    res=pltpu.VMEM((ROWS, HEADS * HEAD), BF),
    hidden=pltpu.VMEM((TALL, HEAD), BF),
    pos=pltpu.VMEM((1, ROWS), jnp.int32),
    gain_in=pltpu.VMEM((32, HEAD), BF),
    ids=pltpu.VMEM((2, ROWS), jnp.int32),
    kept=pltpu.VMEM((2, ROWS), jnp.int32),
    gates=pltpu.VMEM((2, ROWS), F32),
    local_sem=pltpu.SemaphoreType.DMA((12,)),
)
SCRATCH = ATTEND_SCRATCH | EXPERT_SCRATCH | LOCAL_SCRATCH


def layer_kernel(res, q, key, value, pos, gain, wg, wu, wd, ids, kept, gates, out_ref, *scratch):
    s = types.SimpleNamespace(**dict(zip(SCRATCH, scratch)))
    place = Place()
    mine = place.x * 2 + place.a
    moves = dict(
        k=(key, s.kg.at[mine]),
        v=(value, s.vg.at[mine]),
        q=(q, s.qg.at[place.z]),
        pos=(pos, s.pos),
        ids=(ids, s.ids),
        kept=(kept, s.kept),
        gates=(gates, s.gates),
        gain=(gain, s.gain_in),
        res=(res, s.res),
        wg=(wg.at[0], s.w_gate),
        wu=(wu.at[0], s.w_up),
        wd=(wd.at[0], s.w_down),
    )
    local = {
        name: pltpu.make_async_copy(src, dst, s.local_sem.at[i])
        for i, (name, (src, dst)) in enumerate(moves.items())
    }
    for copy in local.values():
        copy.start()
    greet(place)

    for name in ("pos",):
        local[name].wait()

    def aside():
        for name in ("ids", "kept", "gates", "gain", "res"):
            local[name].wait()
        tables(s)

    attended, settle = attention(place, s, local, aside)
    tall = []
    for h in range(HEADS):
        res_h = s.res[:, h * HEAD : (h + 1) * HEAD].astype(F32)
        tall.append((res_h + attended[h * ROWS : (h + 1) * ROWS]).astype(BF))
    hidden = jnp.concatenate(tall, axis=0)
    s.hidden[...] = hidden
    weights = [local[name] for name in ("wg", "wu", "wd")]
    mixed, drain = experts(place, hidden, weights, s)
    for h in range(HEADS):
        rows = slice(h * ROWS, (h + 1) * ROWS)
        out_ref[:, h * HEAD : (h + 1) * HEAD] = (s.hidden[rows].astype(F32) + mixed[rows]).astype(BF)
    settle()
    drain()


def body(
    residual_in,
    queries,
    context_key_cache,
    context_value_cache,
    query_pos,
    norm_gain,
    w_gate,
    w_up,
    w_down,
    expert_ids,
    kept_choices,
    gate_weights,
):
    any_spec = pl.BlockSpec(memory_space=pl.ANY)
    return pl.pallas_call(
        layer_kernel,
        out_shape=jax.ShapeDtypeStruct((ROWS, HEADS * HEAD), BF),
        in_specs=[any_spec] * 12,
        out_specs=pl.BlockSpec(memory_space=pltpu.VMEM),
        scratch_shapes=list(SCRATCH.values()),
        compiler_params=pltpu.CompilerParams(
            collective_id=0, has_side_effects=True, vmem_limit_bytes=56 * 2**20
        ),
        name="layer",
    )(
        residual_in,
        queries,
        context_key_cache,
        context_value_cache,
        query_pos.reshape(1, ROWS),
        norm_gain.reshape(32, HEAD),
        w_gate,
        w_up,
        w_down,
        expert_ids.T,
        kept_choices.T,
        gate_weights.T,
    )


def solution(mesh):
    in_specs = (
        P("ctx", "exp"),
        P("ctx", "exp"),
        P("ctx", "exp"),
        P("ctx", "exp"),
        P("ctx"),
        P(),
        P("exp", "ctx", None),
        P("exp", "ctx", None),
        P("exp", "ctx", None),
        P("ctx", None),
        P("ctx", None),
        P("ctx", None),
    )
    out_specs = P("ctx", "exp")
    return jax.shard_map(body, mesh=mesh, in_specs=in_specs, out_specs=out_specs, check_vma=False)
```

```python
import math
import types

import jax
import jax.numpy as jnp
from jax import lax
from jax.experimental import pallas as pl
from jax.experimental.pallas import tpu as pltpu
from jax.sharding import PartitionSpec as P

BF = jnp.bfloat16
F32 = jnp.float32
MESH = pl.DeviceIdType.MESH
NT = (((1,), (1,)), ((), ()))
NN = (((1,), (0,)), ((), ()))
HEAD = 128
ROWS = 64
HEADS = 4
TALL = ROWS * HEADS
KEYS = 1024
MODEL = 4096
HIDDEN = 448
EXPERTS = 8
SLOTS = 12
PIECE = SLOTS * HEADS
WIDE = EXPERTS * HEAD
NEG = -1e30
EPS = 1e-05
DIRECT = (2, 3)
STRAIGHT = (0, 1)
SCALE = HEAD ** (-0.5) * math.log2(math.e)


class Place:
    def __init__(self):
        self.me = lax.axis_index("ctx")
        self.e = lax.axis_index("exp")
        self.z = lax.div(self.me, 8)
        self.x = lax.rem(lax.div(self.me, 2), 4)
        self.a = lax.rem(self.me, 2)
        z = self.z
        self.zk = [z, z + 1 - 2 * lax.rem(z, 2), z + 2 - 4 * lax.div(z, 2), 3 - z]
        self.xr = [self.x] + [lax.rem(self.x + r, 4) for r in (1, 2, 3)]
        self.sib = self.spot(self.z, self.x, 1 - self.a)
        self.right = self.spot(self.z, self.xr[1], self.a)
        self.left = self.spot(self.z, self.xr[3], self.a)
        self.far = self.spot(self.z, self.xr[2], self.a)
        self.ek = [lax.rem(self.e + j, EXPERTS) for j in range(EXPERTS)]

    def spot(self, z, x, a):
        return z * 8 + x * 2 + a

    def piece(self, k, r, a):
        return self.spot(self.zk[k], self.xr[r], a)

    def column(self, k):
        return self.spot(self.zk[k], self.x, self.a)


class Mail:
    def __init__(self, place, sems):
        self.place, self.sems, self.used, self.open = place, sems, 0, []

    def ship(self, ref, at, to_ref, to, recv, recv_at, ctx=None, exp=None):
        target = {name: to_ for name, to_ in (("ctx", ctx), ("exp", exp)) if to_ is not None}
        number = self.used
        self.used += 1

        def make():
            return pltpu.make_async_remote_copy(
                src_ref=ref.at[at],
                dst_ref=to_ref.at[to],
                send_sem=self.sems.at[number],
                recv_sem=recv.at[recv_at],
                device_id=target,
                device_id_type=MESH,
            )

        make().start()
        self.open.append(make)

    def drain(self):
        for make in self.open:
            make().wait_send()
        self.open = []


def landed(slot, recv_sem, place):
    pltpu.make_async_remote_copy(
        src_ref=slot,
        dst_ref=slot,
        send_sem=recv_sem,
        recv_sem=recv_sem,
        device_id={"ctx": place.sib},
        device_id_type=MESH,
    ).wait_recv()


def wide(x, times):
    return jnp.concatenate([x] * times, axis=1)


def upright(line):
    row = lax.broadcasted_iota(jnp.int32, (ROWS, ROWS), 0)
    col = lax.broadcasted_iota(jnp.int32, (ROWS, ROWS), 1)
    return jnp.sum(jnp.where(row == col, line, 0.0), axis=1, keepdims=True)


def greet(place):
    barrier = pltpu.get_barrier_semaphore()
    peers = [{"ctx": c} for c in (place.sib, place.right, place.left, place.far)]
    peers += [
        {"ctx": place.column(k), "exp": place.ek[j]}
        for k in range(4)
        for j in range(EXPERTS)
        if k or j
    ]
    for peer in peers:
        pl.semaphore_signal(barrier, inc=1, device_id=peer, device_id_type=MESH)
    pl.semaphore_wait(barrier, len(peers))


def attention(place, s, local, aside):
    z, a = place.z, place.a
    mail = Mail(place, s.kv_send)
    units = [[x * 2, x * 2 + 1] for x in place.xr]
    own = [lax.select(a == 0, u[0], u[1]) for u in units]
    other = [lax.select(a == 0, u[1], u[0]) for u in units]
    mine = own[0]
    order = [own[0], other[0], own[3], own[1], other[3], other[1], own[2], other[2]]

    downs = [place.spot(z - k, place.x, a) for k in range(4)]
    ups = [z + k for k in range(4)]

    def q_copy(k):
        return pltpu.make_async_remote_copy(
            src_ref=s.qg.at[z],
            dst_ref=s.qg.at[z],
            send_sem=s.q_send.at[k],
            recv_sem=s.q_recv.at[z],
            device_id={"ctx": downs[k]},
            device_id_type=MESH,
        )

    def send(ref, sem, u, *targets):
        for target in targets:
            mail.ship(ref, u, ref, u, sem, u, ctx=target)

    def first_half(u):
        return (u, pl.ds(0, KEYS // 2))

    def last_half(u):
        return (u, pl.ds(KEYS // 2, KEYS // 2))

    def got_k(u):
        landed(s.kg.at[u], s.k_recv.at[u], place)

    def got_v(u):
        landed(s.vg.at[u], s.v_recv.at[u], place)

    local["k"].wait()
    send(s.kg, s.k_recv, mine, place.right, place.left, place.sib)
    local["q"].wait()
    for k in (1, 2, 3):

        @pl.when(z >= k)
        def _(k=k):
            q_copy(k).start()

    local["v"].wait()
    send(s.vg, s.v_recv, mine, place.right, place.left, place.sib)

    s.peak[...] = jnp.full((4 * TALL, HEAD), NEG, F32)
    s.acc[...] = jnp.zeros((4 * TALL, 2 * HEAD), F32)

    def prepare(zq):
        for h in range(HEADS):
            at = pl.ds(pl.multiple_of(zq * TALL + h * ROWS, ROWS), ROWS)
            s.q2[at, :] = s.qg[zq, :, h * HEAD : (h + 1) * HEAD]

    def update(rows, u, pos_col=None):
        scores = lax.dot_general(s.q2[rows], s.kg[u], NT, preferred_element_type=F32)
        if pos_col is not None:
            key = lax.broadcasted_iota(jnp.int32, (TALL, KEYS), 1).astype(F32)
            scores = jnp.where(key <= pos_col, scores, NEG)
        old = s.peak[rows]
        new = jnp.maximum(old, jnp.max(scores, axis=1, keepdims=True))
        probs = jnp.exp2((scores - wide(new, KEYS // HEAD)) * SCALE)
        shrink = jnp.exp2((old - new) * SCALE)
        lanes = sum(probs[:, i : i + HEAD] for i in range(0, KEYS, HEAD))
        add = jnp.dot(probs.astype(BF), s.vg[u], preferred_element_type=F32)
        s.acc[rows, :HEAD] = s.acc[rows, :HEAD] * shrink + add
        s.acc[rows, HEAD:] = s.acc[rows, HEAD:] * shrink + lanes
        s.peak[rows] = new

    prepare(z)
    here = pl.ds(pl.multiple_of(z * TALL, TALL), TALL)
    pos = s.pos[...].astype(F32) - (place.me * KEYS).astype(F32)
    update(here, mine, jnp.concatenate([upright(pos)] * HEADS, axis=0))
    for k in (1, 2, 3):

        @pl.when(z + k <= 3)
        def _(k=k):
            landed(s.qg.at[ups[k]], s.q_recv.at[ups[k]], place)
            prepare(ups[k])

    def arrivals(n):
        if n == 1:
            got_k(other[0])
            got_v(other[0])
        elif n == 2:
            aside()
            got_k(own[3])
            mail.ship(s.kg, first_half(own[3]), s.kg, first_half(own[3]), s.k_recv, own[3], ctx=place.right)
            send(s.kg, s.k_recv, own[3], place.sib)
            got_k(own[1])
            mail.ship(s.kg, last_half(own[1]), s.kg, last_half(own[1]), s.k_half, own[1], ctx=place.left)
            send(s.kg, s.k_recv, own[1], place.sib)
            got_v(own[1])
            mail.ship(s.vg, last_half(own[1]), s.vg, last_half(own[1]), s.v_half, own[1], ctx=place.left)
            send(s.vg, s.v_recv, own[1], place.sib)
            got_v(own[3])
            mail.ship(s.vg, first_half(own[3]), s.vg, first_half(own[3]), s.v_recv, own[3], ctx=place.right)
            send(s.vg, s.v_recv, own[3], place.sib)
        elif n == 4:
            got_k(other[3])
            got_v(other[3])
        elif n == 5:
            got_k(other[1])
            got_v(other[1])
        elif n == 6:
            far = own[2]
            landed(s.kg.at[first_half(far)], s.k_recv.at[far], place)
            landed(s.kg.at[last_half(far)], s.k_half.at[far], place)
            send(s.kg, s.k_recv, far, place.sib)
            landed(s.vg.at[first_half(far)], s.v_recv.at[far], place)
            landed(s.vg.at[last_half(far)], s.v_half.at[far], place)
            send(s.vg, s.v_recv, far, place.sib)
        elif n == 7:
            got_k(other[2])
            got_v(other[2])

    def step(i, carry):
        for n in (1, 2, 4, 5, 6, 7):

            @pl.when(i == n)
            def _(n=n):
                arrivals(n)

        u = order[0]
        for n in range(1, 8):
            u = jnp.where(i == n, order[n], u)
        first = z + (u >= mine).astype(jnp.int32)
        for n in range(4):

            @pl.when(first == n)
            def _(n=n):
                update(slice(n * TALL, 4 * TALL), u)

        return carry

    lax.fori_loop(0, 8, step, 0)

    eye_r = lax.broadcasted_iota(jnp.int32, (HEAD, HEAD), 0)
    eye_c = lax.broadcasted_iota(jnp.int32, (HEAD, HEAD), 1)
    eye = eye_r == eye_c

    def back(zq):
        def one(src, dst, send, recv):
            return pltpu.make_async_remote_copy(
                src_ref=src.at[zq],
                dst_ref=dst.at[z],
                send_sem=send.at[zq],
                recv_sem=recv.at[z],
                device_id={"ctx": place.spot(zq, place.x, a)},
                device_id_type=MESH,
            )

        return (
            one(s.o_out, s.o_in, s.o_send, s.o_recv),
            one(s.l_out, s.l_in, s.l_send, s.l_recv),
        )

    def finish(i, carry):
        zq = 3 - i
        rows = pl.ds(pl.multiple_of(zq * TALL, TALL), TALL)
        total = jnp.sum(s.acc[rows, HEAD:], axis=1, keepdims=True)
        s.o_out[zq] = (s.acc[rows, :HEAD] / total).astype(BF)
        level = s.peak[rows] * SCALE + jnp.log2(total)
        for half in range(2):
            block = level[half * HEAD : (half + 1) * HEAD]
            s.l_out[zq, half : half + 1, :] = jnp.sum(
                jnp.where(eye, block, 0.0), axis=0, keepdims=True
            )
        for copy in back(zq):
            copy.start()
        return carry

    lax.fori_loop(0, 3 - z, finish, 0)

    s.level[...] = s.peak[here] * SCALE
    s.mix[...] = s.acc[here, :HEAD]
    s.mass[...] = jnp.sum(s.acc[here, HEAD:], axis=1, keepdims=True) + jnp.zeros((TALL, HEAD), F32)
    for k in (1, 2, 3):

        @pl.when(z >= k)
        def _(k=k):
            zs = z - k
            landed(s.o_in.at[zs], s.o_recv.at[zs], place)
            landed(s.l_in.at[zs], s.l_recv.at[zs], place)
            spread = []
            for half in range(2):
                line = s.l_in[zs, half : half + 1, :]
                spread.append(jnp.sum(jnp.where(eye, line, 0.0), axis=1, keepdims=True))
            level = jnp.concatenate(spread, axis=0) + jnp.zeros((TALL, HEAD), F32)
            old = s.level[...]
            new = jnp.maximum(old, level)
            shrink, weight = jnp.exp2(old - new), jnp.exp2(level - new)
            s.mix[...] = s.mix[...] * shrink + weight * s.o_in[zs].astype(F32)
            s.mass[...] = s.mass[...] * shrink + weight
            s.level[...] = new

    def settle():
        for k in (1, 2, 3):

            @pl.when(z >= k)
            def _(k=k):
                q_copy(k).wait_send()

        def last(i, carry):
            for copy in back(3 - i):
                copy.wait_send()
            return carry

        lax.fori_loop(0, 3 - z, last, 0)
        mail.drain()

    return s.mix[...] / s.mass[...], settle


ATTEND_SCRATCH = dict(
    kg=pltpu.VMEM((8, KEYS, HEAD), BF),
    vg=pltpu.VMEM((8, KEYS, HEAD), BF),
    qg=pltpu.VMEM((4, ROWS, HEADS * HEAD), BF),
    q2=pltpu.VMEM((4 * TALL, HEAD), BF),
    peak=pltpu.VMEM((4 * TALL, HEAD), F32),
    acc=pltpu.VMEM((4 * TALL, 2 * HEAD), F32),
    level=pltpu.VMEM((TALL, HEAD), F32),
    mix=pltpu.VMEM((TALL, HEAD), F32),
    mass=pltpu.VMEM((TALL, HEAD), F32),
    o_out=pltpu.VMEM((4, TALL, HEAD), BF),
    o_in=pltpu.VMEM((4, TALL, HEAD), BF),
    l_out=pltpu.VMEM((4, 8, HEAD), F32),
    l_in=pltpu.VMEM((4, 8, HEAD), F32),
    kv_send=pltpu.SemaphoreType.DMA((16,)),
    q_send=pltpu.SemaphoreType.DMA((4,)),
    q_recv=pltpu.SemaphoreType.DMA((4,)),
    k_recv=pltpu.SemaphoreType.DMA((8,)),
    v_recv=pltpu.SemaphoreType.DMA((8,)),
    k_half=pltpu.SemaphoreType.DMA((8,)),
    v_half=pltpu.SemaphoreType.DMA((8,)),
    o_send=pltpu.SemaphoreType.DMA((4,)),
    o_recv=pltpu.SemaphoreType.DMA((4,)),
    l_send=pltpu.SemaphoreType.DMA((4,)),
    l_recv=pltpu.SemaphoreType.DMA((4,)),
)


def steps(index, edges):
    return sum((index >= edge).astype(jnp.int32) for edge in edges)


def slot_columns(ids_ref, kept_ref):
    lane = lax.broadcasted_iota(jnp.int32, (ROWS, HEAD), 1)
    flags = []
    for k in range(2):
        ids = upright(ids_ref[k : k + 1, :].astype(F32))
        kept = upright(kept_ref[k : k + 1, :].astype(F32))
        flags.append(((ids == lane.astype(F32)) & (kept == 1.0)).astype(F32))
    before = (
        lax.broadcasted_iota(jnp.int32, (ROWS, ROWS), 1)
        < lax.broadcasted_iota(jnp.int32, (ROWS, ROWS), 0)
    ).astype(F32)
    columns = []
    passed = jnp.zeros((1, HEAD), F32)
    for flag in flags:
        rank = passed + jnp.dot(before, flag, preferred_element_type=F32)
        passed = passed + jnp.sum(flag, axis=0, keepdims=True)
        slot = flag * (lane.astype(F32) * SLOTS + rank + 1.0)
        columns.append(jnp.sum(slot, axis=1, keepdims=True) - 1.0)
    return columns


def slot_and_head(index):
    expert = steps(index, range(PIECE, EXPERTS * PIECE, PIECE))
    within = index - expert * PIECE
    head = steps(within, range(SLOTS, PIECE, SLOTS))
    return (expert * SLOTS + within - head * SLOTS).astype(F32), head


def pick_rows(columns):
    shape = (EXPERTS * PIECE, TALL)
    slot, head = slot_and_head(lax.broadcasted_iota(jnp.int32, shape, 0))
    lane = lax.broadcasted_iota(jnp.int32, (ROWS, TALL), 1)
    group = steps(lane, range(ROWS, TALL, ROWS))
    same = lax.broadcasted_iota(jnp.int32, (ROWS, TALL), 0) == lane - group * ROWS
    hit = jnp.zeros(shape, F32)
    for column in columns:
        line = jnp.sum(jnp.where(same, column, 0.0), axis=0, keepdims=True)
        hit = hit + (line == slot).astype(F32)
    lanes = lax.broadcasted_iota(jnp.int32, shape, 1)
    hit = jnp.where(steps(lanes, range(ROWS, TALL, ROWS)) == head, hit, 0.0)
    return hit.astype(BF)


def place_rows(column):
    shape = (TALL, EXPERTS * PIECE)
    slot, head = slot_and_head(lax.broadcasted_iota(jnp.int32, shape, 1))
    tall = jnp.concatenate([column] * HEADS, axis=0)
    rows = lax.broadcasted_iota(jnp.int32, shape, 0)
    hit = (slot == tall) & (steps(rows, range(ROWS, TALL, ROWS)) == head)
    return hit.astype(F32).astype(BF)


def swap_matrix():
    side = 4 * PIECE
    row = lax.broadcasted_iota(jnp.int32, (side, side), 0)
    col = lax.broadcasted_iota(jnp.int32, (side, side), 1)
    first = steps(row, (PIECE, 2 * PIECE, 3 * PIECE))
    within = row - first * PIECE
    second = steps(within, (SLOTS, 2 * SLOTS, 3 * SLOTS))
    slot = within - second * SLOTS
    return (col == second * PIECE + first * SLOTS + slot).astype(F32).astype(BF)


def tables(s):
    columns = slot_columns(s.ids, s.kept)
    s.take[...] = pick_rows(columns)
    for k in range(2):
        s.spread[k] = place_rows(columns[k])
    s.swap[...] = swap_matrix()
    part = lax.broadcasted_iota(jnp.int32, (PIECE, HEAD), 0)
    part = steps(part, (SLOTS, 2 * SLOTS, 3 * SLOTS))
    for f in range(EXPERTS):
        gain = s.gain_in[f * HEADS : f * HEADS + 1, :].astype(F32)
        for h in range(1, HEADS):
            at = f * HEADS + h
            gain = jnp.where(part >= h, s.gain_in[at : at + 1, :].astype(F32), gain)
        s.gain[f] = gain


def experts(place, hidden, weights, s):
    a, e = place.a, place.e
    mail = Mail(place, s.send)

    chosen = jnp.dot(s.take[...], hidden, preferred_element_type=F32).astype(BF)
    for j in range(EXPERTS):
        s.pick[j] = chosen[j * PIECE : (j + 1) * PIECE]
    for j in range(1, EXPERTS):
        to = place.ek[j]
        mail.ship(s.pick, to, s.picked, e, s.picked_recv, e, exp=to)
    s.picked[e] = s.pick[e]
    ring = lax.broadcasted_iota(jnp.int32, (PIECE, PIECE), 0)
    ring = ring - SLOTS * steps(ring, (SLOTS, 2 * SLOTS, 3 * SLOTS))
    lap = lax.broadcasted_iota(jnp.int32, (PIECE, PIECE), 1)
    lap = lap - SLOTS * steps(lap, (SLOTS, 2 * SLOTS, 3 * SLOTS))
    alike = (ring == lap).astype(F32)
    for j in range(1, EXPERTS):
        f = place.ek[j]
        landed(s.picked.at[f], s.picked_recv.at[f], place)

    squares = jnp.zeros((PIECE, HEAD), F32)
    for f in range(EXPERTS):
        x = s.picked[f].astype(F32)
        squares = squares + x * x
    squares = jnp.sum(squares, axis=1, keepdims=True) + jnp.zeros((PIECE, HEAD), F32)
    total = jnp.dot(alike, squares, precision=lax.Precision.HIGHEST, preferred_element_type=F32)
    scale = lax.rsqrt(total / MODEL + EPS)
    me = place.me
    for f in range(EXPERTS):
        s.rows[me, :, f * HEAD : (f + 1) * HEAD] = (
            s.picked[f].astype(F32) * scale * s.gain[f]
        ).astype(BF)

    def forward(slot, *targets):
        for target in targets:
            mail.ship(s.rows, slot, s.rows, slot, s.rows_recv, slot, ctx=target)

    def got(k, r, core):
        slot = place.piece(k, r, core)
        landed(s.rows.at[slot], s.rows_recv.at[slot], place)
        return slot

    forward(me, place.column(2), place.column(1))

    def fan(k):
        slot = me if k == 0 else got(k, 0, a)
        if k == 2:
            forward(slot, place.column(1))
        forward(slot, place.right, place.left)
        if k in DIRECT:
            forward(slot, place.far)
        forward(slot, place.sib)

    def relay(k):
        slot = got(k, 3, a)
        if k % 2 == 0 and k not in DIRECT:
            forward(slot, place.right)
        forward(slot, place.sib)
        slot = got(k, 1, a)
        if k % 2 == 1 and k not in DIRECT:
            forward(slot, place.left)
        forward(slot, place.sib)

    def end(k):
        forward(got(k, 2, a), place.sib)

    def gather_siblings(k):
        for r in range(4):
            got(k, r, 1 - a)

    def groups(k):
        return [[(r, core) for r in pair_of for core in range(2)] for pair_of in ((2, 1), (3, 0))]

    def arrange(ks):
        for m, k in enumerate(ks):
            for n, group in enumerate(groups(k)):
                slots = [place.piece(k, r, core) for r, core in group]
                stack = jnp.concatenate([s.rows[slot] for slot in slots], axis=0)
                turned = jnp.dot(s.swap[...], stack, preferred_element_type=F32).astype(BF)
                top = (2 * m + n) * PIECE
                for h in range(HEADS):
                    for f in range(EXPERTS):
                        at = (f * HEADS + h) * HEAD
                        s.x[top : top + PIECE, at : at + HEAD] = turned[
                            h * PIECE : (h + 1) * PIECE, f * HEAD : (f + 1) * HEAD
                        ]

    def middle(task):
        s.g[...] = lax.dot_general(s.x[...], s.w_gate[...], NT, preferred_element_type=F32)
        task()
        u = lax.dot_general(s.x[...], s.w_up[...], NT, preferred_element_type=F32)
        g = s.g[...]
        s.act[...] = (g / (1.0 + jnp.exp(-g)) * u).astype(BF)

    def down(task):
        for at in range(0, MODEL, 1024):
            cols = slice(at, at + 1024)
            s.y[:, cols] = jnp.dot(s.act[...], s.w_down[:, cols], preferred_element_type=F32).astype(BF)
            if at == 1024:
                task()

    def hand_over(m, k):
        for n, group in enumerate(groups(k)):
            top = (2 * m + n) * PIECE
            tall = []
            for h in range(HEADS):
                at = [(f * HEADS + h) * HEAD for f in range(EXPERTS)]
                tall.append(
                    jnp.concatenate([s.y[top : top + PIECE, i : i + HEAD] for i in at], axis=1)
                )
            stack = jnp.concatenate(tall, axis=0)
            turned = jnp.dot(s.swap[...], stack, preferred_element_type=F32).astype(BF)
            for p, (r, core) in enumerate(group):
                s.sums[place.piece(k, r, core)] = turned[p * PIECE : (p + 1) * PIECE]
            for r in dict.fromkeys(r for r, _ in group):
                slot, to = place.piece(k, r, 1 - a), k * 4 + r
                mail.ship(s.sums, slot, s.beside, to, s.beside_recv, to, ctx=place.sib)

    def pair(k, r, *more):
        n = k * 4 + r
        landed(s.beside.at[n], s.beside_recv.at[n], place)
        total = s.sums[place.piece(k, r, a)].astype(F32) + s.beside[n].astype(F32)
        for ref, recv in more:
            landed(ref, recv, place)
            total = total + ref[...].astype(F32)
        slot = place.piece(k, r, a)
        s.sums[slot] = total.astype(BF)
        return slot

    def reduce_far(k):
        src = pair(k, 2)
        if k in STRAIGHT:
            mail.ship(s.sums, src, s.from_far, k, s.far_recv, k, ctx=place.far)
        else:
            target = place.right if k % 2 == 0 else place.left
            mail.ship(s.sums, src, s.relayed, k, s.relayed_recv, k, ctx=target)

    def reduce_near(k, joined):
        if k in STRAIGHT:
            todo = () if joined else (1, 3)
        else:
            todo = (1 if (k % 2 == 0) == joined else 3,)
        more = ((s.relayed.at[k], s.relayed_recv.at[k]),) if joined else ()
        for r in todo:
            src = pair(k, r, *more)
            if r == 1:
                mail.ship(s.sums, src, s.from_left, k, s.left_recv, k, ctx=place.right)
            else:
                mail.ship(s.sums, src, s.from_right, k, s.right_recv, k, ctx=place.left)

    def reduce_own(k):
        sides = ((s.from_left.at[k], s.left_recv.at[k]), (s.from_right.at[k], s.right_recv.at[k]))
        if k in STRAIGHT:
            sides += ((s.from_far.at[k], s.far_recv.at[k]),)
        total = s.sums[pair(k, 0, *sides)]
        for f in range(EXPERTS):
            s.done[k, f] = total[:, f * HEAD : (f + 1) * HEAD]
        for j in reversed(range(EXPERTS)):
            to = place.ek[j]
            if k or j:
                where = dict(ctx=place.column(k), exp=to)
                mail.ship(s.done, (k, to), s.home, (k, e), s.home_recv, k * EXPERTS + e, **where)
            else:
                s.home[0, e] = s.done[0, e]

    def work(ks, *tasks):
        for k in ks:
            gather_siblings(k)
        arrange(ks)
        if ks[0] == 0:
            for copy in weights:
                copy.wait()
        middle(tasks[0])
        tasks[1]()
        down(tasks[2])
        for m, k in reversed(list(enumerate(ks))):
            hand_over(m, k)

    def send_first(*ks):
        for k in ks:
            reduce_far(k)
        for k in ks:
            reduce_near(k, False)

    def idle():
        return None

    fan(0)
    fan(1)
    relay(0)
    fan(2)
    relay(1)
    fan(3)
    end(0)
    end(1)
    relay(2)
    work((0, 1), lambda: relay(3), lambda: end(2), idle)
    end(3)
    send_first(1, 0)
    work((2, 3), idle, idle, idle)
    send_first(3, 2)
    reduce_near(1, True)
    reduce_near(0, True)
    reduce_near(3, True)
    reduce_near(2, True)
    reduce_own(1)
    reduce_own(0)
    reduce_own(3)
    reduce_own(2)
    gates = [
        jnp.concatenate([upright(s.gates[k : k + 1, :])] * HEADS, axis=0) for k in range(2)
    ]
    def home_in(k):
        for j in range(EXPERTS):
            if k or j:
                f = place.ek[j]
                landed(s.home.at[k, f], s.home_recv.at[k * EXPERTS + f], place)

    home_in(1)
    home_in(0)
    early = [s.home[0, j].astype(F32) + s.home[1, j].astype(F32) for j in range(EXPERTS)]
    home_in(3)
    home_in(2)
    back = jnp.concatenate(
        [(early[j] + (s.home[2, j].astype(F32) + s.home[3, j].astype(F32))).astype(BF) for j in range(EXPERTS)],
        axis=0,
    )
    mixed = jnp.zeros((TALL, HEAD), F32)
    for k in range(2):
        mixed = mixed + gates[k] * jnp.dot(s.spread[k], back, preferred_element_type=F32)
    return mixed, mail.drain


def piece_buffers(count):
    return pltpu.VMEM((count, PIECE, WIDE), BF)


EXPERT_SCRATCH = dict(
    w_gate=pltpu.VMEM((HIDDEN, MODEL), BF),
    w_up=pltpu.VMEM((HIDDEN, MODEL), BF),
    w_down=pltpu.VMEM((HIDDEN, MODEL), BF),
    take=pltpu.VMEM((EXPERTS * PIECE, TALL), BF),
    swap=pltpu.VMEM((4 * PIECE, 4 * PIECE), BF),
    gain=pltpu.VMEM((EXPERTS, PIECE, HEAD), F32),
    pick=pltpu.VMEM((EXPERTS, PIECE, HEAD), BF),
    picked=pltpu.VMEM((EXPERTS, PIECE, HEAD), BF),
    spread=pltpu.VMEM((2, TALL, EXPERTS * PIECE), BF),
    rows=piece_buffers(32),
    x=pltpu.VMEM((4 * PIECE, MODEL), BF),
    g=pltpu.VMEM((4 * PIECE, HIDDEN), F32),
    act=pltpu.VMEM((4 * PIECE, HIDDEN), BF),
    y=pltpu.VMEM((4 * PIECE, MODEL), BF),
    sums=piece_buffers(32),
    beside=piece_buffers(16),
    relayed=piece_buffers(4),
    from_left=piece_buffers(4),
    from_right=piece_buffers(4),
    from_far=piece_buffers(4),
    done=pltpu.VMEM((4, EXPERTS, PIECE, HEAD), BF),
    home=pltpu.VMEM((4, EXPERTS, PIECE, HEAD), BF),
    send=pltpu.SemaphoreType.DMA((112,)),
    picked_recv=pltpu.SemaphoreType.DMA((EXPERTS,)),
    rows_recv=pltpu.SemaphoreType.DMA((32,)),
    beside_recv=pltpu.SemaphoreType.DMA((16,)),
    relayed_recv=pltpu.SemaphoreType.DMA((4,)),
    left_recv=pltpu.SemaphoreType.DMA((4,)),
    right_recv=pltpu.SemaphoreType.DMA((4,)),
    far_recv=pltpu.SemaphoreType.DMA((4,)),
    home_recv=pltpu.SemaphoreType.DMA((4 * EXPERTS,)),
)


LOCAL_SCRATCH = dict(
    res=pltpu.VMEM((ROWS, HEADS * HEAD), BF),
    hidden=pltpu.VMEM((TALL, HEAD), BF),
    pos=pltpu.VMEM((1, ROWS), jnp.int32),
    gain_in=pltpu.VMEM((32, HEAD), BF),
    ids=pltpu.VMEM((2, ROWS), jnp.int32),
    kept=pltpu.VMEM((2, ROWS), jnp.int32),
    gates=pltpu.VMEM((2, ROWS), F32),
    local_sem=pltpu.SemaphoreType.DMA((12,)),
)
SCRATCH = ATTEND_SCRATCH | EXPERT_SCRATCH | LOCAL_SCRATCH


def layer_kernel(res, q, key, value, pos, gain, wg, wu, wd, ids, kept, gates, out_ref, *scratch):
    s = types.SimpleNamespace(**dict(zip(SCRATCH, scratch)))
    place = Place()
    mine = place.x * 2 + place.a
    moves = dict(
        k=(key, s.kg.at[mine]),
        v=(value, s.vg.at[mine]),
        q=(q, s.qg.at[place.z]),
        pos=(pos, s.pos),
        ids=(ids, s.ids),
        kept=(kept, s.kept),
        gates=(gates, s.gates),
        gain=(gain, s.gain_in),
        res=(res, s.res),
        wg=(wg.at[0], s.w_gate),
        wu=(wu.at[0], s.w_up),
        wd=(wd.at[0], s.w_down),
    )
    local = {
        name: pltpu.make_async_copy(src, dst, s.local_sem.at[i])
        for i, (name, (src, dst)) in enumerate(moves.items())
    }
    for copy in local.values():
        copy.start()
    greet(place)

    for name in ("pos",):
        local[name].wait()

    def aside():
        for name in ("ids", "kept", "gates", "gain", "res"):
            local[name].wait()
        tables(s)

    attended, settle = attention(place, s, local, aside)
    tall = []
    for h in range(HEADS):
        res_h = s.res[:, h * HEAD : (h + 1) * HEAD].astype(F32)
        tall.append((res_h + attended[h * ROWS : (h + 1) * ROWS]).astype(BF))
    hidden = jnp.concatenate(tall, axis=0)
    s.hidden[...] = hidden
    weights = [local[name] for name in ("wg", "wu", "wd")]
    mixed, drain = experts(place, hidden, weights, s)
    for h in range(HEADS):
        rows = slice(h * ROWS, (h + 1) * ROWS)
        out_ref[:, h * HEAD : (h + 1) * HEAD] = (s.hidden[rows].astype(F32) + mixed[rows]).astype(BF)
    settle()
    drain()


def body(
    residual_in,
    queries,
    context_key_cache,
    context_value_cache,
    query_pos,
    norm_gain,
    w_gate,
    w_up,
    w_down,
    expert_ids,
    kept_choices,
    gate_weights,
):
    any_spec = pl.BlockSpec(memory_space=pl.ANY)
    return pl.pallas_call(
        layer_kernel,
        out_shape=jax.ShapeDtypeStruct((ROWS, HEADS * HEAD), BF),
        in_specs=[any_spec] * 12,
        out_specs=pl.BlockSpec(memory_space=pltpu.VMEM),
        scratch_shapes=list(SCRATCH.values()),
        compiler_params=pltpu.CompilerParams(
            collective_id=0, has_side_effects=True, vmem_limit_bytes=56 * 2**20
        ),
        name="layer",
    )(
        residual_in,
        queries,
        context_key_cache,
        context_value_cache,
        query_pos.reshape(1, ROWS),
        norm_gain.reshape(32, HEAD),
        w_gate,
        w_up,
        w_down,
        expert_ids.T,
        kept_choices.T,
        gate_weights.T,
    )


def solution(mesh):
    in_specs = (
        P("ctx", "exp"),
        P("ctx", "exp"),
        P("ctx", "exp"),
        P("ctx", "exp"),
        P("ctx"),
        P(),
        P("exp", "ctx", None),
        P("exp", "ctx", None),
        P("exp", "ctx", None),
        P("ctx", None),
        P("ctx", None),
        P("ctx", None),
    )
    out_specs = P("ctx", "exp")
    return jax.shard_map(body, mesh=mesh, in_specs=in_specs, out_specs=out_specs, check_vma=False)
```
